512 devices in a mesh: outer: 16 (over y, z_lo), inner: 32 (over z_hi, x, core).
Axes of the slice: x: 4, y: 4, z: 16 (z_hi: 4, z_lo: 4; z = z_hi * 4 + z_lo), core: 2. Of those that a mesh axis runs over, the one named last changes fastest.
Arguments:
- queries: bfloat16 [4096, 2048], P('inner', 'outer'), may hold values from -7.5 to 7.5
- keys: bfloat16 [4096, 2048], P('inner', 'outer'), may hold values from -4 to 4
- values: bfloat16 [4096, 2048], P('inner', 'outer'), may hold values from -6 to 6
- w_out: bfloat16 [2048, 4096], P('outer'), may hold values from -0.5 to 0.5
- grad_out: bfloat16 [4096, 4096], P('inner', 'outer'), may hold values from -1.5 to 1.5
Outputs:
- output: bfloat16 [4096, 4096], P('inner', 'outer')
- grad_queries: bfloat16 [4096, 2048], P('inner', 'outer')
- grad_keys: bfloat16 [4096, 2048], P('inner', 'outer')
- grad_values: bfloat16 [4096, 2048], P('inner', 'outer')
- grad_w_out: float32 [2048, 4096], P('outer', 'inner')
The draws below stay inside these ranges and needn't reach their ends.
All inputs are finite; a program needn't handle non-finite values.
Results may differ from the reference program's by a relative error of at most 0.04.
Values may be sent and summed in bfloat16 or wider, within the bound.
No kernel may reach another device: no remote copies, remote signals or barrier semaphores. Data moves between devices by JAX's collectives and lax.ppermute only.
A program may use at most 64 MiB of HBM per device.

```python
import math
import jax
import jax.numpy as jnp
from jax import lax

HEADS = 16
HDIM = 128
D = 4096
SEQ = 4096
N_OUTER = 16


def draw_queries(key, part):
    key = jax.random.fold_in(key, 11)
    drawn = jnp.clip(2.0 * jax.random.normal(key, (SEQ, HEADS * HDIM), jnp.float32), -7.5, 7.5)
    return drawn.astype(jnp.bfloat16)


def draw_keys(key, part):
    key = jax.random.fold_in(key, 12)
    drawn = jnp.clip(jax.random.normal(key, (SEQ, HEADS * HDIM), jnp.float32), -4.0, 4.0)
    return drawn.astype(jnp.bfloat16)


def raised(result, own_key, source, target, blocks, factor):
    owner, partner = [(jnp.arange(result.shape[axis_at]) // (result.shape[axis_at] // blocks)).reshape([-1 if axis == axis_at else 1 for axis in range(result.ndim)]) for axis_at in (source, target)]
    chosen = jax.random.permutation(own_key, blocks)[partner]
    strong = (owner == chosen) | (owner == (partner + blocks // 2) % blocks)
    return jnp.where(strong, factor * result, result)


def block_levels(key, dims, split, least, high):
    factor_of = 1.0
    for axis_at, parts in split:
        steps = jax.random.uniform(jax.random.fold_in(jax.random.fold_in(key, 6), axis_at), (parts,), jnp.float32, least / len(split), high / len(split))
        factor_of = factor_of * jnp.repeat(jnp.exp(steps), dims[axis_at] // parts).reshape((-1,) + (1,) * (len(dims) - 1 - axis_at))
    return factor_of


def bell_draw(stream_key, shape, scale, reach, split=(), kind=jnp.bfloat16):
    values = jax.random.normal(stream_key, shape, jnp.float32) * scale
    if len(split) > 0:
        values = block_levels(stream_key, shape, split, -0.22, 0.18) * values
    return jnp.clip(values, min=-reach, max=reach).astype(kind)


def gaussian_with(rng, extent, scale, bound, cuts, heavy, kind=jnp.bfloat16):
    values = scale * jax.random.normal(rng, extent, jnp.float32)
    if cuts:
        values = values * block_levels(rng, extent, cuts, -0.22, 0.18)
    return jnp.clip(raised(values, jax.random.fold_in(rng, 3), *heavy), -bound, bound).astype(kind)


def setup_inputs(seed: int = 0) -> dict:
    splits = jax.random.split(jax.random.key(seed), 6)
    return {
        "queries": draw_queries(jax.random.fold_in(splits[5], 71), 0),
        "keys": draw_keys(jax.random.fold_in(splits[5], 71), 0),
        "values": bell_draw(splits[2], (SEQ, HEADS * HDIM), 1.0, 6.0, ((0, 32), (1, 16))),
        "w_out": bell_draw(splits[3], (HEADS * HDIM, D), HDIM ** -0.5, 0.5, ((0, 16),)),
        "grad_out": gaussian_with(splits[4], (SEQ, D), 0.25, 1.5, ((0, 32), (1, 16)), (0, 1, 32, 2.75)),
    }


def head_pass(query_head, key_head, value_head, grad_head):
    score_scale = HDIM ** -0.5
    block_rows = math.gcd(SEQ, 1024)
    block_count = SEQ // block_rows

    def advance(running_state, block_index):
        key_grad, value_grad = running_state
        anchor = (block_index * block_rows).astype(jnp.int32)
        query_block = lax.dynamic_slice_in_dim(query_head, anchor, block_rows, 0)
        grad_block = lax.dynamic_slice_in_dim(grad_head, anchor, block_rows, 0)
        scores = jnp.dot(query_block, key_head.T, preferred_element_type=jnp.float32) * score_scale
        row_max = jnp.max(scores, axis=1, keepdims=True)
        shifted = jnp.exp(scores - row_max)
        totals = jnp.sum(shifted, axis=1, keepdims=True)
        weights = shifted.astype(jnp.bfloat16)
        attention = (jnp.dot(weights, value_head, preferred_element_type=jnp.float32) / totals).astype(jnp.bfloat16)
        log_totals = row_max + jnp.log(totals)
        row_dots = jnp.sum(grad_block.astype(jnp.float32) * attention.astype(jnp.float32), axis=1, keepdims=True)
        probs = jnp.exp(scores - log_totals)
        dprobs = jnp.dot(grad_block, value_head.T, preferred_element_type=jnp.float32)
        dscores = probs * (dprobs - row_dots)
        probs_low = probs.astype(jnp.bfloat16)
        dscores_low = dscores.astype(jnp.bfloat16)
        query_grad = (jnp.dot(dscores_low, key_head, preferred_element_type=jnp.float32) * score_scale).astype(jnp.bfloat16)
        key_grad = key_grad + jnp.dot(dscores_low.T, query_block, preferred_element_type=jnp.float32)
        value_grad = value_grad + jnp.dot(probs_low.T, grad_block, preferred_element_type=jnp.float32)
        return (key_grad, value_grad), (attention, query_grad)

    empty = jnp.zeros((SEQ, HDIM), jnp.float32)
    finals, blocks = lax.scan(advance, (empty, empty), jnp.arange(block_count, dtype=jnp.int32))
    attention = blocks[0].reshape(SEQ, HDIM)
    query_grad = blocks[1].reshape(SEQ, HDIM)
    key_grad = (finals[0] * score_scale).astype(jnp.bfloat16)
    value_grad = finals[1].astype(jnp.bfloat16)
    return attention, query_grad, key_grad, value_grad


def split_heads(array):
    return array.reshape(SEQ, HEADS, HDIM).transpose(1, 0, 2)


def join_heads(array):
    return array.transpose(1, 0, 2).reshape(SEQ, HEADS * HDIM)


def project_groups(attention, w_out):
    group_cols = (HEADS // N_OUTER) * HDIM
    attn_groups = attention.reshape(SEQ, N_OUTER, group_cols).transpose(1, 0, 2)
    weight_groups = w_out.reshape(N_OUTER, group_cols, D)

    def add_group(total, pair):
        term = jnp.dot(pair[0], pair[1], preferred_element_type=jnp.float32).astype(jnp.bfloat16)
        term = lax.optimization_barrier(term)
        return total + term.astype(jnp.float32), None

    total, unused = lax.scan(add_group, jnp.zeros((SEQ, D), jnp.float32), (attn_groups, weight_groups))
    return total.astype(jnp.bfloat16)


def reference(queries, keys, values, w_out, grad_out):
    grad_attention = jnp.dot(grad_out, w_out.T, preferred_element_type=jnp.float32).astype(jnp.bfloat16)
    stacked = (split_heads(queries), split_heads(keys), split_heads(values), split_heads(grad_attention))
    results = lax.map(lambda group: head_pass(group[0], group[1], group[2], group[3]), stacked)
    attention = join_heads(results[0])
    output = project_groups(attention, w_out)
    grad_w_out = jnp.dot(attention.T, grad_out, preferred_element_type=jnp.float32)
    return (output, join_heads(results[1]), join_heads(results[2]), join_heads(results[3]), grad_w_out)
```

```python
import functools

import jax
import jax.numpy as jnp
from jax import lax
from jax.experimental import pallas as pl
from jax.experimental.pallas import tpu as pltpu
from jax.sharding import Mesh, PartitionSpec as P

HDIM = 128
BLK = 128
SCALE = HDIM ** (-0.5)
F32 = jnp.float32
BF16 = jnp.bfloat16


def dot(a, b, dims=((1,), (0,))):
    return lax.dot_general(a, b, (dims, ((), ())), preferred_element_type=F32)


def forward_kernel(q_ref, *refs):
    pieces, (w_ref, attn_ref, lse_ref, out_ref, s_ref) = refs[:8], refs[8:]
    q = q_ref[...]
    width = 4 * BLK
    top = jnp.full((BLK, BLK), -jnp.inf, F32)
    for j, piece in enumerate(pieces):
        k = piece[:, 0].reshape(width, HDIM)
        s = dot(q, k, ((1,), (1,))) * SCALE
        s_ref[:, j * width : (j + 1) * width] = s
        for t in range(4):
            top = jnp.maximum(top, s[:, t * BLK : (t + 1) * BLK])
    row_max = jnp.max(top, axis=1, keepdims=True)
    sums = jnp.zeros((BLK, BLK), F32)
    acc = jnp.zeros((BLK, HDIM), F32)
    for j, piece in enumerate(pieces):
        p = jnp.exp(s_ref[:, j * width : (j + 1) * width] - row_max)
        for t in range(4):
            sums = sums + p[:, t * BLK : (t + 1) * BLK]
        v = piece[:, 1].reshape(width, HDIM)
        acc = acc + dot(p.astype(BF16), v)
    totals = jnp.sum(sums, axis=1, keepdims=True)
    attn = (acc / totals).astype(BF16)
    attn_ref[...] = attn
    lse_ref[...] = jnp.broadcast_to(row_max + jnp.log(totals), (BLK, BLK))
    for o in range(16):
        out_ref[o] = dot(attn, w_ref[:, o * 256 : (o + 1) * 256]).astype(BF16)


def backward_kernel(core_ref, q_ref, *refs):
    pieces = refs[:8]
    w_ref, cot_ref, attn_ref, lse_ref, dq_ref, own_ref, oth_ref = refs[8:]
    core = core_ref[0]
    x_pos = core_ref[1]
    width = 4 * BLK
    q = q_ref[...]
    attn = attn_ref[...]
    grad = jnp.zeros((BLK, HDIM), F32)
    for o in range(16):
        grad = grad + dot(cot_ref[o], w_ref[:, o * 256 : (o + 1) * 256], ((1,), (1,)))
    dattn = grad.astype(BF16)
    dots = jnp.sum(dattn.astype(F32) * attn.astype(F32), axis=1, keepdims=True)
    lse = lse_ref[...][:, :1]
    q_t = q.T
    dattn_t = dattn.T
    attn_t = attn.T
    dq = jnp.zeros((BLK, HDIM), F32)
    for j, piece in enumerate(pieces):
        k = piece[:, 0].reshape(width, HDIM)
        v = piece[:, 1].reshape(width, HDIM)
        s = dot(q, k, ((1,), (1,))) * SCALE
        p = jnp.exp(s - lse)
        dp = dot(dattn, v, ((1,), (1,)))
        ds = (p * (dp - dots)).astype(BF16)
        dq = dq + dot(ds, k)
        dk_t = dot(q_t, ds).astype(BF16)
        dv_t = dot(dattn_t, p.astype(BF16)).astype(BF16)
        ref = own_ref if j < 4 else oth_ref
        for z in range(4):
            ref[j % 4, z, 0] = dk_t[:, z * BLK : (z + 1) * BLK]
            ref[j % 4, z, 1] = dv_t[:, z * BLK : (z + 1) * BLK]
    dq_ref[...] = (dq * SCALE).astype(BF16)
    first = core == 0
    for r in range(4):
        x_dst = lax.rem(x_pos + (4 - r), 4)
        for z in range(4):
            g = dot(attn_t, cot_ref[z * 4 + x_dst])
            left, right = g[:, :BLK], g[:, BLK:]
            own_ref[r, z, 2] = jnp.where(first, left, right).astype(BF16)
            oth_ref[r, z, 2] = jnp.where(first, right, left).astype(BF16)


def rot(shift):
    return [(i, (i + shift) % 4) for i in range(4)]


SWAP = [(0, 1), (1, 0)]
VMEM = pl.BlockSpec(memory_space=pltpu.VMEM)
SMEM = pl.BlockSpec(memory_space=pltpu.SMEM)


def body(queries, keys, values, w_out, grad_out):
    kv = jnp.stack([keys, values])
    cot = lax.all_gather(grad_out, "zl", axis=0)
    kv, cot = lax.optimization_barrier((kv, cot))
    cot = lax.all_gather(cot, "y", axis=0, tiled=True)
    kv0 = lax.all_gather(kv, "zh", axis=0)
    own = [kv0] + [lax.ppermute(kv0, "x", rot(k)) for k in (1, 2, 3)]
    other = [lax.ppermute(piece, "c", SWAP) for piece in own]
    pieces = own + other
    shape = jax.ShapeDtypeStruct
    attn, lse, partial_out = pl.pallas_call(
        forward_kernel,
        out_shape=(
            shape((BLK, HDIM), BF16),
            shape((BLK, BLK), F32),
            shape((16, BLK, 256), BF16),
        ),
        in_specs=[VMEM] * 10,
        out_specs=(VMEM,) * 3,
        scratch_shapes=[pltpu.VMEM((BLK, 32 * BLK), F32)],
        compiler_params=pltpu.CompilerParams(vmem_limit_bytes=40 << 20),
        cost_estimate=pl.CostEstimate(
            flops=6 * BLK * BLK * 4096, bytes_accessed=5 << 20, transcendentals=BLK * 4096
        ),
        name="forward",
    )(queries, *pieces, w_out)
    out = lax.psum_scatter(partial_out, "y", scatter_dimension=0, tiled=True)
    place = jnp.stack([lax.axis_index("c"), lax.axis_index("x")]).astype(jnp.int32)
    dq, pay_own, pay_oth = pl.pallas_call(
        backward_kernel,
        out_shape=(
            shape((BLK, HDIM), BF16),
            shape((4, 4, 3, BLK, BLK), BF16),
            shape((4, 4, 3, BLK, BLK), BF16),
        ),
        in_specs=[SMEM] + [VMEM] * 13,
        out_specs=(VMEM,) * 3,
        compiler_params=pltpu.CompilerParams(vmem_limit_bytes=40 << 20),
        cost_estimate=pl.CostEstimate(
            flops=14 * BLK * BLK * 4096, bytes_accessed=9 << 20, transcendentals=BLK * 4096
        ),
        name="backward",
    )(place, queries, *pieces, w_out, cot, attn, lse)
    got = lax.ppermute(pay_oth, "c", SWAP)
    parts = [(pay_own[r].astype(F32) + got[r].astype(F32)).astype(BF16) for r in range(4)]
    total = parts[0].astype(F32)
    for r in (1, 2, 3):
        total = total + lax.ppermute(parts[r], "x", rot(4 - r)).astype(F32)
    total = total.astype(BF16)
    total = jnp.sum(
        lax.all_to_all(total, "zh", 0, 0, tiled=True).astype(F32), axis=0
    )
    dk = (total[0].T * SCALE).astype(BF16)
    dv = total[1].T.astype(BF16)
    dw = total[2]
    out = lax.all_to_all(out, "zl", 0, 0, tiled=True)
    out = jnp.sum(out.astype(F32), axis=0).astype(BF16)
    return out, dq, dk, dv, dw


def solution(mesh):
    fine = Mesh(mesh.devices.reshape(4, 4, 4, 4, 2), ("y", "zl", "zh", "x", "c"))
    outer, inner = ("y", "zl"), ("zh", "x", "c")
    spread = P(inner, outer)
    return jax.shard_map(
        body,
        mesh=fine,
        in_specs=(spread, spread, spread, P(outer, None), spread),
        out_specs=(spread, spread, spread, spread, P(outer, inner)),
        check_vma=False,
    )
```

```python
import functools

import jax
import jax.numpy as jnp
from jax import lax
from jax.experimental import pallas as pl
from jax.experimental.pallas import tpu as pltpu
from jax.sharding import Mesh, PartitionSpec as P

HDIM = 128
BLK = 128
SCALE = HDIM ** (-0.5)
F32 = jnp.float32
BF16 = jnp.bfloat16


def dot(a, b, dims=((1,), (0,))):
    return lax.dot_general(a, b, (dims, ((), ())), preferred_element_type=F32)


def block_of(place_ref, y_step, zl_step):
    y = lax.rem(place_ref[1] + (4 + y_step), 4)
    zl = lax.rem(place_ref[2] + (4 + zl_step), 4)
    return y, zl


def pack_kernel(place_ref, q_ref, k_ref, v_ref, grad_ref, kv_ref, gift_ref, mine_ref):
    for z in range(4):
        kv_ref[z, 0] = k_ref[...]
        kv_ref[z, 1] = v_ref[...]
    first = place_ref[0] == 0
    left, right = grad_ref[:, :BLK], grad_ref[:, BLK:]
    mine_ref[...] = jnp.where(first, left, right)
    gift_ref[:, :HDIM] = q_ref[...]
    gift_ref[:, HDIM:] = jnp.where(first, right, left)


def forward_kernel(place_ref, q_ref, other_ref, kv_ref, w_ref, cot0, cot1, cot2, cot3, part_ref, s_ref):
    grad = jnp.zeros((2 * BLK, HDIM), F32)
    for r, cot_ref in enumerate((cot0, cot1, cot2, cot3)):
        for t in range(4):
            y, zl = block_of(place_ref, -r, -t)
            start = pl.multiple_of((y * 4 + zl) * 256 + place_ref[0] * BLK, BLK)
            grad = grad + dot(cot_ref[t], w_ref[:, pl.ds(start, BLK)], ((1,), (1,)))
    part_ref[:, :HDIM] = grad
    q = jnp.concatenate([q_ref[...], other_ref[:, :HDIM]], axis=0)
    width = 4 * BLK
    top = jnp.full((2 * BLK, BLK), -jnp.inf, F32)
    for j in range(4):
        k = kv_ref[j, :, 0].reshape(width, HDIM)
        s = dot(q, k, ((1,), (1,))) * SCALE
        s_ref[:, j * width : (j + 1) * width] = s
        for t in range(4):
            top = jnp.maximum(top, s[:, t * BLK : (t + 1) * BLK])
    row_max = jnp.max(top, axis=1, keepdims=True)
    sums = jnp.zeros((2 * BLK, BLK), F32)
    acc = jnp.zeros((2 * BLK, HDIM), F32)
    for j in range(4):
        p = jnp.exp(s_ref[:, j * width : (j + 1) * width] - row_max)
        for t in range(4):
            sums = sums + p[:, t * BLK : (t + 1) * BLK]
        v = kv_ref[j, :, 1].reshape(width, HDIM)
        acc = acc + dot(p.astype(BF16), v)
    totals = jnp.sum(sums, axis=1, keepdims=True)
    part_ref[:, HDIM : 2 * HDIM] = acc / totals
    part_ref[:, 2 * HDIM :] = jnp.broadcast_to(row_max + jnp.log(totals), (2 * BLK, BLK))


def merge_kernel(place_ref, mine_ref, theirs_ref, w_ref, grad_ref, attn_ref, lse_ref, dots_ref, *out_refs):
    for half in range(2):
        rows = slice(half * BLK, (half + 1) * BLK)
        swapped = slice((1 - half) * BLK, (2 - half) * BLK)
        grad = (mine_ref[rows, :HDIM] + theirs_ref[swapped, :HDIM]).astype(BF16)
        a, b = mine_ref[rows, 2 * HDIM :], theirs_ref[swapped, 2 * HDIM :]
        top = jnp.maximum(a, b)
        lse = top + jnp.log(jnp.exp(a - top) + jnp.exp(b - top))
        attn = mine_ref[rows, HDIM : 2 * HDIM] * jnp.exp(a - lse)
        attn = attn + theirs_ref[swapped, HDIM : 2 * HDIM] * jnp.exp(b - lse)
        attn = attn.astype(BF16)
        dots = jnp.sum(grad.astype(F32) * attn.astype(F32), axis=1, keepdims=True)
        grad_ref[rows, :] = grad
        attn_ref[rows, :] = attn
        lse_ref[rows, :] = lse
        dots_ref[rows, :] = jnp.broadcast_to(dots, (BLK, BLK))
    attn = attn_ref[:BLK, :]
    for r, out_ref in enumerate(out_refs):
        for t in range(4):
            y, zl = block_of(place_ref, r, t)
            cols = pl.ds(pl.multiple_of((y * 4 + zl) * 256, 256), 256)
            out_ref[t] = dot(attn, w_ref[:, cols]).astype(BF16)


def backward_kernel(
    place_ref,
    q_ref,
    other_ref,
    kv_ref,
    cot0,
    cot1,
    cot2,
    cot3,
    grad_ref,
    attn_ref,
    lse_ref,
    dots_ref,
    dq_own_ref,
    dq_oth_ref,
    pay_ref,
):
    width = 4 * BLK
    q = jnp.concatenate([q_ref[...], other_ref[:, :HDIM]], axis=0)
    grad = grad_ref[...]
    lse = lse_ref[:, :1]
    dots = dots_ref[:, :1]
    q_t = q.T
    grad_t = grad.T
    attn_t = attn_ref[...].T
    dq = jnp.zeros((2 * BLK, HDIM), F32)
    for j in range(4):
        k = kv_ref[j, :, 0].reshape(width, HDIM)
        v = kv_ref[j, :, 1].reshape(width, HDIM)
        s = dot(q, k, ((1,), (1,))) * SCALE
        p = jnp.exp(s - lse)
        dp = dot(grad, v, ((1,), (1,)))
        ds = (p * (dp - dots)).astype(BF16)
        dq = dq + dot(ds, k)
        dk_t = dot(q_t, ds).astype(BF16)
        dv_t = dot(grad_t, p.astype(BF16)).astype(BF16)
        for z in range(4):
            pay_ref[j, z, 0] = dk_t[:, z * BLK : (z + 1) * BLK]
            pay_ref[j, z, 1] = dv_t[:, z * BLK : (z + 1) * BLK]
    dq_own_ref[...] = dq[:BLK]
    dq_oth_ref[...] = dq[BLK:]
    for r, cot_ref in enumerate((cot0, cot1, cot2, cot3)):
        for t in range(4):
            z, x = block_of(place_ref, -r, -t)
            pay_ref[x, z, 2] = dot(attn_t, cot_ref[t]).astype(BF16)


def finish_kernel(parts_ref, dk_ref, dv_ref, dw_ref):
    total = jnp.sum(parts_ref[...].astype(F32), axis=0)
    dk_ref[...] = (total[0] * SCALE).T.astype(BF16)
    dv_ref[...] = total[1].T.astype(BF16)
    dw_ref[...] = total[2]


FIRST, SECOND = "zl", "y"
VMEM = pl.BlockSpec(memory_space=pltpu.VMEM)
SMEM = pl.BlockSpec(memory_space=pltpu.SMEM)
shape = jax.ShapeDtypeStruct


def exchange(blocks, axis):
    return lax.all_to_all(blocks, axis, 0, 0, tiled=True)


def spread_over(block, axis):
    return exchange(jnp.broadcast_to(block[None], (4,) + block.shape), axis)


def shift(block, axis, by):
    return lax.ppermute(block, axis, [(i, (i + by) % 4) for i in range(4)])


def swap(block):
    return lax.ppermute(block, "c", [(0, 1), (1, 0)])


def add_all(blocks):
    total = blocks[0].astype(F32)
    for block in blocks[1:]:
        total = total + block.astype(F32)
    return total.astype(BF16)


def call(kernel, name, out_shape, in_specs, limit, flops, nbytes, exps=0, scratch=()):
    return pl.pallas_call(
        kernel,
        out_shape=out_shape,
        in_specs=in_specs,
        out_specs=jax.tree.map(lambda _: VMEM, out_shape),
        scratch_shapes=scratch,
        compiler_params=pltpu.CompilerParams(vmem_limit_bytes=limit << 20),
        cost_estimate=pl.CostEstimate(flops=flops, bytes_accessed=nbytes, transcendentals=exps),
        name=name,
    )


def body(queries, keys, values, w_out, grad_out):
    unit = BLK * BLK * 4096
    tile = shape((BLK, BLK), BF16)
    pair = shape((2 * BLK, HDIM), BF16)
    wide = shape((2 * BLK, BLK), F32)
    place = jnp.stack([lax.axis_index(a) for a in ("c", "y", "zl")]).astype(jnp.int32)
    kv, gift, mine = call(
        pack_kernel,
        "pack",
        (shape((4, 2, BLK, BLK), BF16), shape((BLK, 2 * BLK), BF16), tile),
        [SMEM] + [VMEM] * 4,
        4,
        0,
        1 << 19,
    )(place, queries, keys, values, grad_out)
    place, kv, mine, gift = lax.optimization_barrier((place, kv, mine, gift))
    other = swap(gift)
    kv = exchange(kv, "zh")
    cot = jnp.concatenate([mine, other[:, BLK:]], axis=0)
    cot = jnp.stack([cot] + [shift(cot, FIRST, k) for k in (1, 2, 3)])
    kv, cot = lax.optimization_barrier((kv, cot))
    kv = spread_over(kv, "x")
    cots = [cot] + [shift(cot, SECOND, k) for k in (2, 1, 3)]
    kv, cots = lax.optimization_barrier((kv, cots))
    cots = [cots[0], cots[2], cots[1], cots[3]]
    part = call(
        forward_kernel,
        "forward",
        shape((2 * BLK, 3 * BLK), F32),
        [SMEM] + [VMEM] * 8,
        8,
        6 * unit,
        5 << 20,
        unit // BLK,
        [pltpu.VMEM((2 * BLK, 16 * BLK), F32)],
    )(place, queries, other, kv, w_out, *cots)
    theirs = swap(part)
    quarter = shape((4, BLK, 256), BF16)
    grad, attn, lse, dots, *outs = call(
        merge_kernel,
        "merge",
        (pair, pair, wide, wide) + (quarter,) * 4,
        [SMEM] + [VMEM] * 3,
        8,
        2 * unit,
        2 << 20,
    )(place, part, theirs, w_out)
    dq, dq_other, pay = call(
        backward_kernel,
        "backward",
        (shape((BLK, HDIM), F32), shape((BLK, HDIM), F32), shape((4, 4, 3, BLK, BLK), BF16)),
        [SMEM] + [VMEM] * 11,
        8,
        12 * unit,
        6 << 20,
        unit // BLK,
    )(place, queries, other, kv, *cots, grad, attn, lse, dots)
    pay, outs = lax.optimization_barrier((pay, outs))
    pay = exchange(pay, "x")
    outs = [outs[0]] + [shift(outs[k], SECOND, k) for k in (2, 1, 3)]
    pay, outs = lax.optimization_barrier((pay, outs))
    pay = add_all([pay[r] for r in range(4)])
    out = add_all(outs)
    pay, out = lax.optimization_barrier((pay, out))
    pay = exchange(pay, "zh")
    out = add_all([out[0]] + [shift(out[k], FIRST, k) for k in (1, 2, 3)])
    dq = ((dq + swap(dq_other)) * SCALE).astype(BF16)
    dk, dv, dw = call(
        finish_kernel, "finish", (tile, tile, shape((BLK, BLK), F32)), [VMEM], 4, 0, 1 << 20
    )(pay)
    return out, dq, dk, dv, dw


def solution(mesh):
    fine = Mesh(mesh.devices.reshape(4, 4, 4, 4, 2), ("y", "zl", "zh", "x", "c"))
    outer, inner = ("y", "zl"), ("zh", "x", "c")
    spread = P(inner, outer)
    return jax.shard_map(
        body,
        mesh=fine,
        in_specs=(spread, spread, spread, P(outer, None), spread),
        out_specs=(spread, spread, spread, spread, P(outer, inner)),
        check_vma=False,
    )
```

```python
import jax
import jax.numpy as jnp
from jax import lax
from jax.experimental import pallas as pl
from jax.experimental.pallas import tpu as pltpu
from jax.sharding import Mesh, PartitionSpec as P

HDIM = 128
BLK = 128
WIDTH = 4 * BLK
SCALE = HDIM ** (-0.5)
F32 = jnp.float32
BF16 = jnp.bfloat16
VMEM = pl.BlockSpec(memory_space=pltpu.VMEM)
SMEM = pl.BlockSpec(memory_space=pltpu.SMEM)
shape = jax.ShapeDtypeStruct


def dot(a, b, dims=((1,), (0,))):
    return lax.dot_general(a, b, (dims, ((), ())), preferred_element_type=F32)


def project_kernel(place_ref, attn_ref, w_ref, *out_refs):
    for r, out_ref in enumerate(out_refs):
        for t in range(4):
            o = lax.bitwise_xor(place_ref[2], r) * 4 + lax.bitwise_xor(place_ref[3], t)
            cols = pl.ds(pl.multiple_of(o * 256, 256), 256)
            out_ref[t] = dot(attn_ref[...], w_ref[:, cols]).astype(BF16)


def forward_kernel(place_ref, q_ref, other_ref, kv0, kv1, kv2, kv3, w_ref, cot_ref, part_ref, s_ref):
    pieces = (kv0, kv1, kv2, kv3)
    grad = jnp.zeros((2 * BLK, HDIM), F32)
    for o in range(16):
        start = pl.multiple_of(o * 256 + place_ref[0] * BLK, BLK)
        grad = grad + dot(cot_ref[o], w_ref[:, pl.ds(start, BLK)], ((1,), (1,)))
    part_ref[:, :HDIM] = grad
    q = jnp.concatenate([q_ref[...], other_ref[0]], axis=0)
    top = jnp.full((2 * BLK, BLK), -jnp.inf, F32)
    for j in range(4):
        k = pieces[j][:, 0].reshape(WIDTH, HDIM)
        s = dot(q, k, ((1,), (1,))) * SCALE
        s_ref[:, j * WIDTH : (j + 1) * WIDTH] = s
        for t in range(4):
            top = jnp.maximum(top, s[:, t * BLK : (t + 1) * BLK])
    row_max = jnp.max(top, axis=1, keepdims=True)
    sums = jnp.zeros((2 * BLK, BLK), F32)
    acc = jnp.zeros((2 * BLK, HDIM), F32)
    for j in range(4):
        p = jnp.exp(s_ref[:, j * WIDTH : (j + 1) * WIDTH] - row_max)
        for t in range(4):
            sums = sums + p[:, t * BLK : (t + 1) * BLK]
        v = pieces[j][:, 1].reshape(WIDTH, HDIM)
        acc = acc + dot(p.astype(BF16), v)
    totals = jnp.sum(sums, axis=1, keepdims=True)
    part_ref[:, HDIM : 2 * HDIM] = acc / totals
    part_ref[:, 2 * HDIM :] = jnp.broadcast_to(row_max + jnp.log(totals), (2 * BLK, BLK))


def merged(mine_ref, theirs_ref, half):
    rows = slice(half * BLK, (half + 1) * BLK)
    swapped = slice((1 - half) * BLK, (2 - half) * BLK)
    grad = (mine_ref[rows, :HDIM] + theirs_ref[swapped, :HDIM]).astype(BF16)
    a, b = mine_ref[rows, 2 * HDIM :], theirs_ref[swapped, 2 * HDIM :]
    top = jnp.maximum(a, b)
    lse = top + jnp.log(jnp.exp(a - top) + jnp.exp(b - top))
    attn = mine_ref[rows, HDIM : 2 * HDIM] * jnp.exp(a - lse)
    attn = (attn + theirs_ref[swapped, HDIM : 2 * HDIM] * jnp.exp(b - lse)).astype(BF16)
    dots = jnp.sum(grad.astype(F32) * attn.astype(F32), axis=1, keepdims=True)
    return grad, attn, lse[:, :1], dots


def backward_kernel(place_ref, q_ref, other_ref, kv0, kv1, kv2, kv3, cot_ref, mine_ref, theirs_ref, *refs):
    pieces = (kv0, kv1, kv2, kv3)
    dq_ref, pay_ref, attn_ref = refs
    halves = [merged(mine_ref, theirs_ref, half) for half in range(2)]
    grad, attn, lse, dots = (jnp.concatenate(pair, axis=0) for pair in zip(*halves))
    attn_ref[...] = halves[0][1]
    q = jnp.concatenate([q_ref[...], other_ref[0]], axis=0)
    q_t = q.T
    grad_t = grad.T
    attn_t = attn.T
    dq = jnp.zeros((2 * BLK, HDIM), F32)
    for j in range(4):
        k = pieces[j][:, 0].reshape(WIDTH, HDIM)
        v = pieces[j][:, 1].reshape(WIDTH, HDIM)
        s = dot(q, k, ((1,), (1,))) * SCALE
        p = jnp.exp(s - lse)
        dp = dot(grad, v, ((1,), (1,)))
        ds = (p * (dp - dots)).astype(BF16)
        dq = dq + dot(ds, k)
        dk_t = dot(q_t, ds).astype(BF16)
        dv_t = dot(grad_t, p.astype(BF16)).astype(BF16)
        x = lax.bitwise_xor(place_ref[1], j)
        for z in range(4):
            pay_ref[x, z, 0] = dk_t[:, z * BLK : (z + 1) * BLK]
            pay_ref[x, z, 1] = dv_t[:, z * BLK : (z + 1) * BLK]
    dq_ref[0] = dq[:BLK]
    dq_ref[1] = dq[BLK:]
    for x in range(4):
        for z in range(4):
            pay_ref[x, z, 2] = dot(attn_t, cot_ref[z * 4 + x]).astype(BF16)


def finish_kernel(parts_ref, dk_ref, dv_ref, dw_ref):
    total = jnp.sum(parts_ref[...].astype(F32), axis=0)
    dk_ref[...] = (total[0] * SCALE).T.astype(BF16)
    dv_ref[...] = total[1].T.astype(BF16)
    dw_ref[...] = total[2]


def exchange(blocks, axis):
    return lax.all_to_all(blocks, axis, 0, 0, tiled=True)


def trade(block, axis, step):
    return lax.ppermute(block, axis, [(i, i ^ step) for i in range(2 if axis == "c" else 4)])


def add_all(blocks):
    total = blocks[0].astype(F32)
    for block in blocks[1:]:
        total = total + block.astype(F32)
    return total


def call(kernel, name, out_shape, in_specs, limit, flops, nbytes, exps=0, scratch=()):
    return pl.pallas_call(
        kernel,
        out_shape=out_shape,
        in_specs=in_specs,
        out_specs=jax.tree.map(lambda _: VMEM, out_shape),
        scratch_shapes=scratch,
        compiler_params=pltpu.CompilerParams(vmem_limit_bytes=limit << 20),
        cost_estimate=pl.CostEstimate(flops=flops, bytes_accessed=nbytes, transcendentals=exps),
        name=name,
    )


def body(queries, keys, values, w_out, grad_out):
    unit = BLK * BLK * 4096
    tile = shape((BLK, BLK), BF16)
    place = jnp.stack([lax.axis_index(a) for a in ("c", "x", "y", "zl")]).astype(jnp.int32)
    place, keys = lax.optimization_barrier((place, keys))
    first = place[0] == 0
    left, right = grad_out[:, :BLK], grad_out[:, BLK:]
    other = trade(jnp.stack([queries, jnp.where(first, right, left)]), "c", 1)
    cot = jnp.concatenate([jnp.where(first, left, right), other[1]], axis=0)
    kv = lax.all_gather(jnp.concatenate([keys, values]), "zh", axis=0, tiled=True)
    kv = kv.reshape(4, 2, BLK, HDIM)
    kv, cot = lax.optimization_barrier((kv, cot))
    cot = exchange(jnp.broadcast_to(cot[None], (16, 2 * BLK, BLK)), ("y", "zl"))
    pieces = [kv] + [trade(kv, "x", r) for r in (1, 2, 3)]
    cot, pieces = lax.optimization_barrier((cot, pieces))
    part = call(
        forward_kernel,
        "forward",
        shape((2 * BLK, 3 * BLK), F32),
        [SMEM] + [VMEM] * 8,
        8,
        6 * unit,
        5 << 20,
        unit // BLK,
        [pltpu.VMEM((2 * BLK, 16 * BLK), F32)],
    )(place, queries, other, *pieces, w_out, cot)
    theirs = trade(part, "c", 1)
    dq, pay, attn = call(
        backward_kernel,
        "backward",
        (shape((2, BLK, HDIM), F32), shape((4, 4, 3, BLK, BLK), BF16), tile),
        [SMEM] + [VMEM] * 9,
        8,
        12 * unit,
        7 << 20,
        unit // BLK,
    )(place, queries, other, *pieces, cot, part, theirs)
    dq, pay, attn = lax.optimization_barrier((dq, pay, attn))
    pay = exchange(pay, "x")
    dq_got = trade(dq[1], "c", 1)
    attn, dq_got = lax.optimization_barrier((attn, dq_got))
    quarter = shape((4, BLK, 256), BF16)
    outs = call(
        project_kernel, "project", (quarter,) * 4, [SMEM] + [VMEM] * 2, 8, 2 * unit, 2 << 20
    )(place, attn, w_out)
    outs = [outs[0]] + [trade(outs[r], "y", r) for r in (1, 2, 3)]
    pay = add_all([pay[r] for r in range(4)]).astype(BF16)
    out = add_all(outs).astype(BF16)
    pay = exchange(pay, "zh")
    out = add_all([out[0]] + [trade(out[t], "zl", t) for t in (1, 2, 3)]).astype(BF16)
    dq = ((dq[0] + dq_got) * SCALE).astype(BF16)
    dk, dv, dw = call(
        finish_kernel, "finish", (tile, tile, shape((BLK, BLK), F32)), [VMEM], 4, 0, 1 << 20
    )(pay)
    return out, dq, dk, dv, dw


def solution(mesh):
    fine = Mesh(mesh.devices.reshape(4, 4, 4, 4, 2), ("y", "zl", "zh", "x", "c"))
    outer, inner = ("y", "zl"), ("zh", "x", "c")
    spread = P(inner, outer)
    return jax.shard_map(
        body,
        mesh=fine,
        in_specs=(spread, spread, spread, P(outer, None), spread),
        out_specs=(spread, spread, spread, spread, P(outer, inner)),
        check_vma=False,
    )
```

```python
import jax
import jax.numpy as jnp
from jax import lax
from jax.experimental import pallas as pl
from jax.experimental.pallas import tpu as pltpu
from jax.sharding import Mesh, PartitionSpec as P

HDIM = 128
BLK = 128
WIDTH = 4 * BLK
SCALE = HDIM ** (-0.5)
F32 = jnp.float32
BF16 = jnp.bfloat16
VMEM = pl.BlockSpec(memory_space=pltpu.VMEM)
SMEM = pl.BlockSpec(memory_space=pltpu.SMEM)
HBM = pl.BlockSpec(memory_space=pltpu.HBM)
shape = jax.ShapeDtypeStruct


def dot(a, b, dims=((1,), (0,))):
    return lax.dot_general(a, b, (dims, ((), ())), preferred_element_type=F32)


def forward_kernel(place_ref, q_ref, other_ref, kv0, kv1, kv2, kv3, w_ref, cot_ref, part_ref, s_ref):
    pieces = (kv0, kv1, kv2, kv3)
    grad = jnp.zeros((2 * BLK, HDIM), F32)
    for o in range(16):
        start = pl.multiple_of(o * 256 + place_ref[0] * BLK, BLK)
        grad = grad + dot(cot_ref[o], w_ref[:, pl.ds(start, BLK)], ((1,), (1,)))
    part_ref[:, :HDIM] = grad
    q = jnp.concatenate([q_ref[...], other_ref[0]], axis=0)
    top = jnp.full((2 * BLK, BLK), -jnp.inf, F32)
    for j in range(4):
        k = pieces[j][:, 0].reshape(WIDTH, HDIM)
        s = dot(q, k, ((1,), (1,))) * SCALE
        s_ref[:, j * WIDTH : (j + 1) * WIDTH] = s
        for t in range(4):
            top = jnp.maximum(top, s[:, t * BLK : (t + 1) * BLK])
    row_max = jnp.max(top, axis=1, keepdims=True)
    sums = jnp.zeros((2 * BLK, BLK), F32)
    acc = jnp.zeros((2 * BLK, HDIM), F32)
    for j in range(4):
        p = jnp.exp(s_ref[:, j * WIDTH : (j + 1) * WIDTH] - row_max)
        for t in range(4):
            sums = sums + p[:, t * BLK : (t + 1) * BLK]
        v = pieces[j][:, 1].reshape(WIDTH, HDIM)
        acc = acc + dot(p.astype(BF16), v)
    totals = jnp.sum(sums, axis=1, keepdims=True)
    part_ref[:, HDIM : 2 * HDIM] = acc / totals
    part_ref[:, 2 * HDIM :] = jnp.broadcast_to(row_max + jnp.log(totals), (2 * BLK, BLK))


def merged(mine_ref, theirs_ref, half):
    rows = slice(half * BLK, (half + 1) * BLK)
    swapped = slice((1 - half) * BLK, (2 - half) * BLK)
    grad = (mine_ref[rows, :HDIM] + theirs_ref[swapped, :HDIM]).astype(BF16)
    a, b = mine_ref[rows, 2 * HDIM :], theirs_ref[swapped, 2 * HDIM :]
    top = jnp.maximum(a, b)
    lse = top + jnp.log(jnp.exp(a - top) + jnp.exp(b - top))
    attn = mine_ref[rows, HDIM : 2 * HDIM] * jnp.exp(a - lse)
    attn = (attn + theirs_ref[swapped, HDIM : 2 * HDIM] * jnp.exp(b - lse)).astype(BF16)
    dots = jnp.sum(grad.astype(F32) * attn.astype(F32), axis=1, keepdims=True)
    return grad, attn, lse[:, :1], dots


def backward_kernel(
    place_ref, q_ref, other_ref, kv0, kv1, kv2, kv3, cot_ref, w_ref, mine_ref, theirs_ref, *refs
):
    pieces = (kv0, kv1, kv2, kv3)
    dq_ref, pay_hbm, *out_hbm, pay_ref, out_ref, sems = refs
    halves = [merged(mine_ref, theirs_ref, half) for half in range(2)]
    grad, attn, lse, dots = (jnp.concatenate(pair, axis=0) for pair in zip(*halves))
    copies = []
    for r in range(4):
        for t in range(4):
            o = lax.bitwise_xor(place_ref[2], t) * 4 + lax.bitwise_xor(place_ref[3], r)
            cols = pl.ds(pl.multiple_of(o * 256, 256), 256)
            out_ref[r, t] = dot(halves[0][1], w_ref[:, cols]).astype(BF16)
        copies.append(pltpu.make_async_copy(out_ref.at[r], out_hbm[r], sems.at[r]))
        copies[r].start()
    q = jnp.concatenate([q_ref[...], other_ref[0]], axis=0)
    q_t = q.T
    grad_t = grad.T
    attn_t = attn.T
    dq = jnp.zeros((2 * BLK, HDIM), F32)
    for j in range(4):
        x = lax.bitwise_xor(place_ref[1], j)
        k = pieces[j][:, 0].reshape(WIDTH, HDIM)
        v = pieces[j][:, 1].reshape(WIDTH, HDIM)
        s = dot(q, k, ((1,), (1,))) * SCALE
        p = jnp.exp(s - lse)
        dp = dot(grad, v, ((1,), (1,)))
        ds = (p * (dp - dots)).astype(BF16)
        dq = dq + dot(ds, k)
        dk_t = dot(q_t, ds).astype(BF16)
        dv_t = dot(grad_t, p.astype(BF16)).astype(BF16)
        for z in range(4):
            pay_ref[j, z, 0] = dk_t[:, z * BLK : (z + 1) * BLK]
            pay_ref[j, z, 1] = dv_t[:, z * BLK : (z + 1) * BLK]
            pay_ref[j, z, 2] = dot(attn_t, cot_ref[z * 4 + x]).astype(BF16)
        copies.append(pltpu.make_async_copy(pay_ref.at[j], pay_hbm.at[x], sems.at[4 + j]))
        copies[4 + j].start()
    dq_ref[0] = dq[:BLK]
    dq_ref[1] = dq[BLK:]
    for copy in copies:
        copy.wait()


def finish_kernel(parts_ref, dk_ref, dv_ref, dw_ref):
    total = jnp.sum(parts_ref[...].astype(F32), axis=0)
    dk_ref[...] = (total[0] * SCALE).T.astype(BF16)
    dv_ref[...] = total[1].T.astype(BF16)
    dw_ref[...] = total[2]


def exchange(blocks, axis):
    return lax.all_to_all(blocks, axis, 0, 0, tiled=True)


def trade(block, axis, step):
    return lax.ppermute(block, axis, [(i, i ^ step) for i in range(2 if axis == "c" else 4)])


def add_all(blocks):
    total = blocks[0].astype(F32)
    for block in blocks[1:]:
        total = total + block.astype(F32)
    return total


def call(kernel, name, out_shape, in_specs, limit, flops, nbytes, exps=0, scratch=(), out_specs=None):
    return pl.pallas_call(
        kernel,
        out_shape=out_shape,
        in_specs=in_specs,
        out_specs=jax.tree.map(lambda _: VMEM, out_shape) if out_specs is None else out_specs,
        scratch_shapes=scratch,
        compiler_params=pltpu.CompilerParams(vmem_limit_bytes=limit << 20),
        cost_estimate=pl.CostEstimate(flops=flops, bytes_accessed=nbytes, transcendentals=exps),
        name=name,
    )


def body(queries, keys, values, w_out, grad_out):
    unit = BLK * BLK * 4096
    tile = shape((BLK, BLK), BF16)
    place = jnp.stack([lax.axis_index(a) for a in ("c", "x", "y", "zl")]).astype(jnp.int32)
    place, keys = lax.optimization_barrier((place, keys))
    first = place[0] == 0
    left, right = grad_out[:, :BLK], grad_out[:, BLK:]
    other = trade(jnp.stack([queries, jnp.where(first, right, left)]), "c", 1)
    cot = jnp.concatenate([jnp.where(first, left, right), other[1]], axis=0)
    kv = lax.all_gather(jnp.concatenate([keys, values]), "zh", axis=0, tiled=True)
    kv = kv.reshape(4, 2, BLK, HDIM)
    kv, cot = lax.optimization_barrier((kv, cot))
    cot = exchange(jnp.broadcast_to(cot[None], (16, 2 * BLK, BLK)), ("y", "zl"))
    pieces = [kv] + [trade(kv, "x", r) for r in (1, 2, 3)]
    cot, pieces = lax.optimization_barrier((cot, pieces))
    part = call(
        forward_kernel,
        "forward",
        shape((2 * BLK, 3 * BLK), F32),
        [SMEM] + [VMEM] * 8,
        8,
        6 * unit,
        5 << 20,
        unit // BLK,
        [pltpu.VMEM((2 * BLK, 16 * BLK), F32)],
    )(place, queries, other, *pieces, w_out, cot)
    theirs = trade(part, "c", 1)
    dq, pay, *outs = call(
        backward_kernel,
        "backward",
        (shape((2, BLK, HDIM), F32), pltpu.HBM((4, 4, 3, BLK, BLK), BF16))
        + (pltpu.HBM((4, BLK, 256), BF16),) * 4,
        [SMEM] + [VMEM] * 10,
        12,
        14 * unit,
        8 << 20,
        unit // BLK,
        [
            pltpu.VMEM((4, 4, 3, BLK, BLK), BF16),
            pltpu.VMEM((4, 4, BLK, 256), BF16),
            pltpu.SemaphoreType.DMA((8,)),
        ],
        (VMEM,) + (HBM,) * 5,
    )(place, queries, other, *pieces, cot, w_out, part, theirs)
    pay, *outs = lax.optimization_barrier((pay, *outs))
    pay = exchange(pay, "x")
    passing = trade(outs[3], "zl", 1)
    near = trade(outs[1], "zl", 1)
    dq_got = trade(dq[1], "c", 1)
    passing, dq_got = lax.optimization_barrier((passing, dq_got))
    far = trade(add_all([outs[2], passing]).astype(BF16), "zl", 2)
    pay = add_all([pay[r] for r in range(4)]).astype(BF16)
    pay = exchange(pay, "zh")
    out = add_all([outs[0], near, far]).astype(BF16)
    out = add_all([out[0]] + [trade(out[t], "y", t) for t in (1, 2, 3)]).astype(BF16)
    dq = ((dq[0] + dq_got) * SCALE).astype(BF16)
    dk, dv, dw = call(
        finish_kernel, "finish", (tile, tile, shape((BLK, BLK), F32)), [VMEM], 4, 0, 1 << 20
    )(pay)
    return out, dq, dk, dv, dw


def solution(mesh):
    fine = Mesh(mesh.devices.reshape(4, 4, 4, 4, 2), ("y", "zl", "zh", "x", "c"))
    outer, inner = ("y", "zl"), ("zh", "x", "c")
    spread = P(inner, outer)
    return jax.shard_map(
        body,
        mesh=fine,
        in_specs=(spread, spread, spread, P(outer, None), spread),
        out_specs=(spread, spread, spread, spread, P(outer, inner)),
        check_vma=False,
    )
```

```python
import jax
import jax.numpy as jnp
from jax import lax
from jax.experimental import pallas as pl
from jax.experimental.pallas import tpu as pltpu
from jax.sharding import Mesh, PartitionSpec as P

HDIM = 128
BLK = 128
WIDTH = 4 * BLK
SCALE = HDIM ** (-0.5)
F32 = jnp.float32
BF16 = jnp.bfloat16
VMEM = pl.BlockSpec(memory_space=pltpu.VMEM)
SMEM = pl.BlockSpec(memory_space=pltpu.SMEM)
HBM = pl.BlockSpec(memory_space=pltpu.HBM)
shape = jax.ShapeDtypeStruct


def dot(a, b, dims=((1,), (0,))):
    return lax.dot_general(a, b, (dims, ((), ())), preferred_element_type=F32)


def pack_kernel(place_ref, q_hbm, k_hbm, v_hbm, grad_hbm, kv_ref, gift_ref, mine_ref, grad_ref, sems):
    copies = [
        pltpu.make_async_copy(grad_hbm, grad_ref, sems.at[0]),
        pltpu.make_async_copy(q_hbm, gift_ref.at[0], sems.at[1]),
        pltpu.make_async_copy(k_hbm, kv_ref.at[pl.ds(0, BLK)], sems.at[2]),
        pltpu.make_async_copy(v_hbm, kv_ref.at[pl.ds(BLK, BLK)], sems.at[3]),
    ]
    for copy in copies:
        copy.start()
    for copy in copies:
        copy.wait()
    first = place_ref[0] == 0
    left, right = grad_ref[:, :BLK], grad_ref[:, BLK:]
    mine_ref[...] = jnp.where(first, left, right)
    gift_ref[1] = jnp.where(first, right, left)


def copies_kernel(mine_ref, other_ref, cot_hbm, pair_ref, sems):
    pair_ref[:BLK] = mine_ref[...]
    pair_ref[BLK:] = other_ref[1]
    copies = [pltpu.make_async_copy(pair_ref, cot_hbm.at[o], sems.at[o]) for o in range(16)]
    for copy in copies:
        copy.start()
    for copy in copies:
        copy.wait()


def cotangent_kernel(place_ref, w_ref, cot_ref, part_in, part_ref):
    grad = jnp.zeros((2 * BLK, HDIM), F32)
    for o in range(16):
        start = pl.multiple_of(o * 256 + place_ref[0] * BLK, BLK)
        grad = grad + dot(cot_ref[o], w_ref[:, pl.ds(start, BLK)], ((1,), (1,)))
    part_ref[:, :HDIM] = grad
    part_ref[:, HDIM:] = part_in[...]


def forward_kernel(q_ref, other_ref, kv0, kv1, kv2, kv3, part_ref, s_ref):
    pieces = (kv0, kv1, kv2, kv3)
    q = jnp.concatenate([q_ref[...], other_ref[0]], axis=0)
    top = jnp.full((2 * BLK, BLK), -jnp.inf, F32)
    for j in range(4):
        k = pieces[j][:, 0].reshape(WIDTH, HDIM)
        s = dot(q, k, ((1,), (1,))) * SCALE
        s_ref[:, j * WIDTH : (j + 1) * WIDTH] = s
        for t in range(4):
            top = jnp.maximum(top, s[:, t * BLK : (t + 1) * BLK])
    row_max = jnp.max(top, axis=1, keepdims=True)
    sums = jnp.zeros((2 * BLK, BLK), F32)
    acc = jnp.zeros((2 * BLK, HDIM), F32)
    for j in range(4):
        p = jnp.exp(s_ref[:, j * WIDTH : (j + 1) * WIDTH] - row_max)
        for t in range(4):
            sums = sums + p[:, t * BLK : (t + 1) * BLK]
        v = pieces[j][:, 1].reshape(WIDTH, HDIM)
        acc = acc + dot(p.astype(BF16), v)
    totals = jnp.sum(sums, axis=1, keepdims=True)
    part_ref[:, :HDIM] = acc / totals
    part_ref[:, HDIM:] = jnp.broadcast_to(row_max + jnp.log(totals), (2 * BLK, BLK))


def merged(mine_ref, theirs_ref, half):
    rows = slice(half * BLK, (half + 1) * BLK)
    swapped = slice((1 - half) * BLK, (2 - half) * BLK)
    grad = (mine_ref[rows, :HDIM] + theirs_ref[swapped, :HDIM]).astype(BF16)
    a, b = mine_ref[rows, 2 * HDIM :], theirs_ref[swapped, 2 * HDIM :]
    top = jnp.maximum(a, b)
    lse = top + jnp.log(jnp.exp(a - top) + jnp.exp(b - top))
    attn = mine_ref[rows, HDIM : 2 * HDIM] * jnp.exp(a - lse)
    attn = (attn + theirs_ref[swapped, HDIM : 2 * HDIM] * jnp.exp(b - lse)).astype(BF16)
    dots = jnp.sum(grad.astype(F32) * attn.astype(F32), axis=1, keepdims=True)
    return grad, attn, lse[:, :1], dots


def backward_kernel(
    place_ref, q_ref, other_ref, kv0, kv1, kv2, kv3, cot_ref, w_ref, mine_ref, theirs_ref, *refs
):
    pieces = (kv0, kv1, kv2, kv3)
    dq_ref, pay_hbm, *out_hbm, pay_ref, out_ref, sems = refs
    halves = [merged(mine_ref, theirs_ref, half) for half in range(2)]
    grad, attn, lse, dots = (jnp.concatenate(pair, axis=0) for pair in zip(*halves))
    copies = []
    for r in range(4):
        for t in range(4):
            o = lax.bitwise_xor(place_ref[2], t) * 4 + lax.bitwise_xor(place_ref[3], r)
            cols = pl.ds(pl.multiple_of(o * 256, 256), 256)
            out_ref[r, t] = dot(halves[0][1], w_ref[:, cols]).astype(BF16)
        copies.append(pltpu.make_async_copy(out_ref.at[r], out_hbm[r], sems.at[r]))
        copies[r].start()
    q = jnp.concatenate([q_ref[...], other_ref[0]], axis=0)
    q_t = q.T
    grad_t = grad.T
    attn_t = attn.T
    dq = jnp.zeros((2 * BLK, HDIM), F32)
    for j in range(4):
        x = lax.bitwise_xor(place_ref[1], j)
        k = pieces[j][:, 0].reshape(WIDTH, HDIM)
        v = pieces[j][:, 1].reshape(WIDTH, HDIM)
        s = dot(q, k, ((1,), (1,))) * SCALE
        p = jnp.exp(s - lse)
        dp = dot(grad, v, ((1,), (1,)))
        ds = (p * (dp - dots)).astype(BF16)
        dq = dq + dot(ds, k)
        dk_t = dot(q_t, ds).astype(BF16)
        dv_t = dot(grad_t, p.astype(BF16)).astype(BF16)
        for z in range(4):
            pay_ref[j, z, 0] = dk_t[:, z * BLK : (z + 1) * BLK]
            pay_ref[j, z, 1] = dv_t[:, z * BLK : (z + 1) * BLK]
            pay_ref[j, z, 2] = dot(attn_t, cot_ref[z * 4 + x]).astype(BF16)
        copies.append(pltpu.make_async_copy(pay_ref.at[j], pay_hbm.at[x], sems.at[4 + j]))
        copies[4 + j].start()
    dq_ref[0] = dq[:BLK]
    dq_ref[1] = dq[BLK:]
    for copy in copies:
        copy.wait()


def finish_kernel(parts_ref, dk_ref, dv_ref, dw_ref):
    total = jnp.sum(parts_ref[...].astype(F32), axis=0)
    dk_ref[...] = (total[0] * SCALE).T.astype(BF16)
    dv_ref[...] = total[1].T.astype(BF16)
    dw_ref[...] = total[2]


def exchange(blocks, axis):
    return lax.all_to_all(blocks, axis, 0, 0, tiled=True)


def trade(block, axis, step):
    return lax.ppermute(block, axis, [(i, i ^ step) for i in range(2 if axis == "c" else 4)])


def in_hbm(block):
    return pltpu.with_memory_space_constraint(block, pltpu.HBM)


def add_all(blocks):
    total = blocks[0].astype(F32)
    for block in blocks[1:]:
        total = total + block.astype(F32)
    return total


def call(kernel, name, out_shape, in_specs, limit, flops, nbytes, exps=0, scratch=(), out_specs=None):
    return pl.pallas_call(
        kernel,
        out_shape=out_shape,
        in_specs=in_specs,
        out_specs=jax.tree.map(lambda _: VMEM, out_shape) if out_specs is None else out_specs,
        scratch_shapes=scratch,
        compiler_params=pltpu.CompilerParams(vmem_limit_bytes=limit << 20),
        cost_estimate=pl.CostEstimate(flops=flops, bytes_accessed=nbytes, transcendentals=exps),
        name=name,
    )


def body(queries, keys, values, w_out, grad_out):
    unit = BLK * BLK * 4096
    tile = shape((BLK, BLK), BF16)
    place = jnp.stack([lax.axis_index(a) for a in ("c", "x", "y", "zl")]).astype(jnp.int32)
    kv, gift, mine = call(
        pack_kernel,
        "pack",
        (shape((2 * BLK, HDIM), BF16), shape((2, BLK, BLK), BF16), tile),
        [SMEM] + [HBM] * 4,
        4,
        0,
        1 << 19,
        scratch=[pltpu.VMEM((BLK, 2 * BLK), BF16), pltpu.SemaphoreType.DMA((4,))],
    )(place, *[in_hbm(block) for block in (queries, keys, values, grad_out)])
    place, kv, gift, mine = lax.optimization_barrier((place, kv, gift, mine))
    other = trade(gift, "c", 1)
    kv = lax.all_gather(kv, "zh", axis=0, tiled=True).reshape(4, 2, BLK, HDIM)
    kv, other = lax.optimization_barrier((kv, other))
    cot = jnp.concatenate([mine, other[1]], axis=0)
    cot = exchange(jnp.broadcast_to(cot[None], (16, 2 * BLK, BLK)), ("y", "zl"))
    pieces = [kv] + [trade(kv, "x", r) for r in (1, 2, 3)]
    part = call(
        forward_kernel,
        "forward",
        shape((2 * BLK, 2 * BLK), F32),
        [VMEM] * 6,
        8,
        4 * unit,
        4 << 20,
        unit // BLK,
        [pltpu.VMEM((2 * BLK, 16 * BLK), F32)],
    )(queries, other, *pieces)
    cot, part = lax.optimization_barrier((cot, part))
    part = call(
        cotangent_kernel,
        "cotangent",
        shape((2 * BLK, 3 * BLK), F32),
        [SMEM] + [VMEM] * 3,
        8,
        2 * unit,
        2 << 20,
    )(place, w_out, cot, part)
    theirs = trade(part, "c", 1)
    dq, pay, *outs = call(
        backward_kernel,
        "backward",
        (shape((2, BLK, HDIM), F32), pltpu.HBM((4, 4, 3, BLK, BLK), BF16))
        + (pltpu.HBM((4, BLK, 256), BF16),) * 4,
        [SMEM] + [VMEM] * 10,
        12,
        14 * unit,
        8 << 20,
        unit // BLK,
        [
            pltpu.VMEM((4, 4, 3, BLK, BLK), BF16),
            pltpu.VMEM((4, 4, BLK, 256), BF16),
            pltpu.SemaphoreType.DMA((8,)),
        ],
        (VMEM,) + (HBM,) * 5,
    )(place, queries, other, *pieces, cot, w_out, part, theirs)
    pay, *outs = lax.optimization_barrier((pay, *outs))
    pay = exchange(pay, "x")
    passing = trade(outs[3], "zl", 1)
    near = trade(outs[1], "zl", 1)
    dq_got = trade(dq[1], "c", 1)
    passing, dq_got = lax.optimization_barrier((passing, dq_got))
    far = trade(add_all([outs[2], passing]).astype(BF16), "zl", 2)
    pay = add_all([pay[r] for r in range(4)]).astype(BF16)
    pay = exchange(pay, "zh")
    out = add_all([outs[0], near, far]).astype(BF16)
    out = add_all([out[0]] + [trade(out[t], "y", t) for t in (1, 2, 3)]).astype(BF16)
    dq = ((dq[0] + dq_got) * SCALE).astype(BF16)
    dk, dv, dw = call(
        finish_kernel, "finish", (tile, tile, shape((BLK, BLK), F32)), [VMEM], 4, 0, 1 << 20
    )(pay)
    return out, dq, dk, dv, dw


def solution(mesh):
    fine = Mesh(mesh.devices.reshape(4, 4, 4, 4, 2), ("y", "zl", "zh", "x", "c"))
    outer, inner = ("y", "zl"), ("zh", "x", "c")
    spread = P(inner, outer)
    return jax.shard_map(
        body,
        mesh=fine,
        in_specs=(spread, spread, spread, P(outer, None), spread),
        out_specs=(spread, spread, spread, spread, P(outer, inner)),
        check_vma=False,
    )
```

```python
import jax
import jax.numpy as jnp
from jax import lax
from jax.experimental import pallas as pl
from jax.experimental.pallas import tpu as pltpu
from jax.sharding import Mesh, PartitionSpec as P

HDIM = 128
BLK = 128
WIDTH = 4 * BLK
SCALE = HDIM ** (-0.5)
F32 = jnp.float32
BF16 = jnp.bfloat16
VMEM = pl.BlockSpec(memory_space=pltpu.VMEM)
SMEM = pl.BlockSpec(memory_space=pltpu.SMEM)
HBM = pl.BlockSpec(memory_space=pltpu.HBM)
shape = jax.ShapeDtypeStruct


def dot(a, b, dims=((1,), (0,))):
    return lax.dot_general(a, b, (dims, ((), ())), preferred_element_type=F32)


def pack_kernel(k_hbm, v_hbm, grad_hbm, kv_ref, grad_ref, sems):
    copies = [
        pltpu.make_async_copy(grad_hbm, grad_ref, sems.at[2]),
        pltpu.make_async_copy(k_hbm, kv_ref.at[pl.ds(0, BLK)], sems.at[0]),
        pltpu.make_async_copy(v_hbm, kv_ref.at[pl.ds(BLK, BLK)], sems.at[1]),
    ]
    for copy in copies:
        copy.start()
    for copy in copies:
        copy.wait()


def cotangent_kernel(place_ref, w_ref, cot_ref, gift_ref):
    core = place_ref[0]
    grad = jnp.zeros((BLK, HDIM), F32)
    for o in range(16):
        cot = cot_ref[o]
        grad = grad + dot(cot, w_ref[:, o * 256 : (o + 1) * 256], ((1,), (1,)))
        gift_ref[1 + o] = jnp.where(core == 0, cot[:, BLK:], cot[:, :BLK])
    gift_ref[0] = grad.astype(BF16)


def forward_kernel(q_ref, other_ref, kv0, kv1, kv2, kv3, part_ref, s_ref):
    pieces = (kv0, kv1, kv2, kv3)
    q = jnp.concatenate([q_ref[...], other_ref[...]], axis=0)
    top = jnp.full((2 * BLK, BLK), -jnp.inf, F32)
    for j in range(4):
        k = pieces[j][:, 0].reshape(WIDTH, HDIM)
        s = dot(q, k, ((1,), (1,))) * SCALE
        s_ref[:, j * WIDTH : (j + 1) * WIDTH] = s
        for t in range(4):
            top = jnp.maximum(top, s[:, t * BLK : (t + 1) * BLK])
    row_max = jnp.max(top, axis=1, keepdims=True)
    sums = jnp.zeros((2 * BLK, BLK), F32)
    acc = jnp.zeros((2 * BLK, HDIM), F32)
    for j in range(4):
        p = jnp.exp(s_ref[:, j * WIDTH : (j + 1) * WIDTH] - row_max)
        for t in range(4):
            sums = sums + p[:, t * BLK : (t + 1) * BLK]
        v = pieces[j][:, 1].reshape(WIDTH, HDIM)
        acc = acc + dot(p.astype(BF16), v)
    totals = jnp.sum(sums, axis=1, keepdims=True)
    part_ref[:, :HDIM] = acc / totals
    part_ref[:, HDIM:] = jnp.broadcast_to(row_max + jnp.log(totals), (2 * BLK, BLK))


def merged(grad, mine_ref, theirs_ref, half):
    rows = slice(half * BLK, (half + 1) * BLK)
    swapped = slice((1 - half) * BLK, (2 - half) * BLK)
    a, b = mine_ref[rows, HDIM:], theirs_ref[swapped, HDIM:]
    top = jnp.maximum(a, b)
    lse = top + jnp.log(jnp.exp(a - top) + jnp.exp(b - top))
    attn = mine_ref[rows, :HDIM] * jnp.exp(a - lse)
    attn = (attn + theirs_ref[swapped, :HDIM] * jnp.exp(b - lse)).astype(BF16)
    dots = jnp.sum(grad.astype(F32) * attn.astype(F32), axis=1, keepdims=True)
    return grad, attn, lse[:, :1], dots


def backward_kernel(
    place_ref, q_ref, other_ref, kv0, kv1, kv2, kv3, cot_ref, w_ref, gift_ref, got_ref, mine_ref, theirs_ref, *refs
):
    pieces = (kv0, kv1, kv2, kv3)
    dq_ref, pay_hbm, *out_hbm, pay_ref, out_ref, sems = refs
    halves = [
        merged(ref[0], mine_ref, theirs_ref, half) for half, ref in enumerate((gift_ref, got_ref))
    ]
    mine = pl.ds(pl.multiple_of(place_ref[0] * BLK, BLK), BLK)
    grad, attn, lse, dots = (jnp.concatenate(pair, axis=0) for pair in zip(*halves))
    copies = []
    for r in range(4):
        for t in range(4):
            o = lax.bitwise_xor(place_ref[2], t) * 4 + lax.bitwise_xor(place_ref[3], r)
            cols = pl.ds(pl.multiple_of(o * 256, 256), 256)
            out_ref[r, t] = dot(halves[0][1], w_ref[:, cols]).astype(BF16)
        copies.append(pltpu.make_async_copy(out_ref.at[r], out_hbm[r], sems.at[r]))
        copies[r].start()
    q = jnp.concatenate([q_ref[...], other_ref[...]], axis=0)
    q_t = q.T
    grad_t = grad.T
    attn_t = attn.T
    dq = jnp.zeros((2 * BLK, HDIM), F32)
    for j in range(4):
        x = lax.bitwise_xor(place_ref[1], j)
        k = pieces[j][:, 0].reshape(WIDTH, HDIM)
        v = pieces[j][:, 1].reshape(WIDTH, HDIM)
        s = dot(q, k, ((1,), (1,))) * SCALE
        p = jnp.exp(s - lse)
        dp = dot(grad, v, ((1,), (1,)))
        ds = (p * (dp - dots)).astype(BF16)
        dq = dq + dot(ds, k)
        dk_t = dot(q_t, ds).astype(BF16)
        dv_t = dot(grad_t, p.astype(BF16)).astype(BF16)
        for z in range(4):
            pay_ref[j, z, 0] = dk_t[:, z * BLK : (z + 1) * BLK]
            pay_ref[j, z, 1] = dv_t[:, z * BLK : (z + 1) * BLK]
            o = z * 4 + x
            cot = jnp.concatenate([cot_ref[o, :, mine], got_ref[1 + o]], axis=0)
            pay_ref[j, z, 2] = dot(attn_t, cot).astype(BF16)
        copies.append(pltpu.make_async_copy(pay_ref.at[j], pay_hbm.at[x], sems.at[4 + j]))
        copies[4 + j].start()
    dq_ref[0] = dq[:BLK]
    dq_ref[1] = dq[BLK:]
    for copy in copies:
        copy.wait()


def finish_kernel(parts_ref, dk_ref, dv_ref, dw_ref):
    total = jnp.sum(parts_ref[...].astype(F32), axis=0)
    dk_ref[...] = (total[0] * SCALE).T.astype(BF16)
    dv_ref[...] = total[1].T.astype(BF16)
    dw_ref[...] = total[2]


def exchange(blocks, axis):
    return lax.all_to_all(blocks, axis, 0, 0, tiled=True)


def trade(block, axis, step):
    return lax.ppermute(block, axis, [(i, i ^ step) for i in range(2 if axis == "c" else 4)])


def in_hbm(block):
    return pltpu.with_memory_space_constraint(block, pltpu.HBM)


def add_all(blocks):
    total = blocks[0].astype(F32)
    for block in blocks[1:]:
        total = total + block.astype(F32)
    return total


def call(kernel, name, out_shape, in_specs, limit, flops, nbytes, exps=0, scratch=(), out_specs=None):
    return pl.pallas_call(
        kernel,
        out_shape=out_shape,
        in_specs=in_specs,
        out_specs=jax.tree.map(lambda _: VMEM, out_shape) if out_specs is None else out_specs,
        scratch_shapes=scratch,
        compiler_params=pltpu.CompilerParams(vmem_limit_bytes=limit << 20),
        cost_estimate=pl.CostEstimate(flops=flops, bytes_accessed=nbytes, transcendentals=exps),
        name=name,
    )


def body(queries, keys, values, w_out, grad_out):
    unit = BLK * BLK * 4096
    tile = shape((BLK, BLK), BF16)
    place = jnp.stack([lax.axis_index(a) for a in ("c", "x", "y", "zl")]).astype(jnp.int32)
    kv, cot = call(
        pack_kernel,
        "pack",
        (shape((2 * BLK, HDIM), BF16), shape((BLK, 2 * BLK), BF16)),
        [HBM] * 3,
        4,
        0,
        1 << 18,
        scratch=[pltpu.SemaphoreType.DMA((3,))],
    )(in_hbm(keys), in_hbm(values), in_hbm(grad_out))
    kv = lax.all_gather(kv, "zh", axis=0, tiled=True).reshape(4, 2, BLK, HDIM)
    kv, gift, cot, place = lax.optimization_barrier((kv, queries, cot, place))
    cot = exchange(jnp.broadcast_to(cot[None], (16, BLK, 2 * BLK)), ("y", "zl"))
    other = trade(gift, "c", 1)
    pieces = [kv] + [trade(kv, "x", r) for r in (1, 2, 3)]
    part = call(
        forward_kernel,
        "forward",
        shape((2 * BLK, 2 * BLK), F32),
        [VMEM] * 6,
        8,
        4 * unit,
        4 << 20,
        unit // BLK,
        [pltpu.VMEM((2 * BLK, 16 * BLK), F32)],
    )(queries, other, *pieces)
    theirs = trade(part, "c", 1)
    cot, theirs = lax.optimization_barrier((cot, theirs))
    gift = call(
        cotangent_kernel,
        "cotangent",
        shape((17, BLK, BLK), BF16),
        [SMEM] + [VMEM] * 2,
        8,
        2 * unit,
        2 << 20,
    )(place, w_out, cot)
    got = trade(gift, "c", 1)
    dq, pay, *outs = call(
        backward_kernel,
        "backward",
        (shape((2, BLK, HDIM), F32), pltpu.HBM((4, 4, 3, BLK, BLK), BF16))
        + (pltpu.HBM((4, BLK, 256), BF16),) * 4,
        [SMEM] + [VMEM] * 12,
        12,
        14 * unit,
        8 << 20,
        unit // BLK,
        [
            pltpu.VMEM((4, 4, 3, BLK, BLK), BF16),
            pltpu.VMEM((4, 4, BLK, 256), BF16),
            pltpu.SemaphoreType.DMA((8,)),
        ],
        (VMEM,) + (HBM,) * 5,
    )(place, queries, other, *pieces, cot, w_out, gift, got, part, theirs)
    pay, *outs = lax.optimization_barrier((pay, *outs))
    pay = exchange(pay, "x")
    passing = trade(outs[3], "zl", 1)
    near = trade(outs[1], "zl", 1)
    dq_got = trade(dq[1], "c", 1)
    passing, dq_got = lax.optimization_barrier((passing, dq_got))
    far = trade(add_all([outs[2], passing]).astype(BF16), "zl", 2)
    pay = add_all([pay[r] for r in range(4)]).astype(BF16)
    pay = exchange(pay, "zh")
    out = add_all([outs[0], near, far]).astype(BF16)
    out = add_all([out[0]] + [trade(out[t], "y", t) for t in (1, 2, 3)]).astype(BF16)
    dq = ((dq[0] + dq_got) * SCALE).astype(BF16)
    dk, dv, dw = call(
        finish_kernel, "finish", (tile, tile, shape((BLK, BLK), F32)), [VMEM], 4, 0, 1 << 20
    )(pay)
    return out, dq, dk, dv, dw


def solution(mesh):
    fine = Mesh(mesh.devices.reshape(4, 4, 4, 4, 2), ("y", "zl", "zh", "x", "c"))
    outer, inner = ("y", "zl"), ("zh", "x", "c")
    spread = P(inner, outer)
    return jax.shard_map(
        body,
        mesh=fine,
        in_specs=(spread, spread, spread, P(outer, None), spread),
        out_specs=(spread, spread, spread, spread, P(outer, inner)),
        check_vma=False,
    )
```

```python
import jax
import jax.numpy as jnp
from jax import lax
from jax.experimental import pallas as pl
from jax.experimental.pallas import tpu as pltpu
from jax.sharding import Mesh, PartitionSpec as P

HDIM = 128
BLK = 128
WIDTH = 4 * BLK
SCALE = HDIM ** (-0.5)
F32 = jnp.float32
BF16 = jnp.bfloat16
VMEM = pl.BlockSpec(memory_space=pltpu.VMEM)
SMEM = pl.BlockSpec(memory_space=pltpu.SMEM)
HBM = pl.BlockSpec(memory_space=pltpu.HBM)
shape = jax.ShapeDtypeStruct


def dot(a, b, dims=((1,), (0,))):
    return lax.dot_general(a, b, (dims, ((), ())), preferred_element_type=F32)


def pack_kernel(k_hbm, v_hbm, grad_hbm, kv_ref, grad_ref, sems):
    copies = [
        pltpu.make_async_copy(grad_hbm, grad_ref, sems.at[2]),
        pltpu.make_async_copy(k_hbm, kv_ref.at[pl.ds(0, BLK)], sems.at[0]),
        pltpu.make_async_copy(v_hbm, kv_ref.at[pl.ds(BLK, BLK)], sems.at[1]),
    ]
    for copy in copies:
        copy.start()
    for copy in copies:
        copy.wait()


def cotangent_kernel(place_ref, w_ref, cot_ref, part_ref, gift_ref):
    core = place_ref[0]
    lane = lax.broadcasted_iota(jnp.int32, (BLK, BLK), 1)
    for half in range(2):
        rows = slice(half * BLK, (half + 1) * BLK)
        values = part_ref[rows, :HDIM]
        high = values.astype(BF16)
        gift_ref[17 + 2 * half] = high
        gift_ref[18 + 2 * half] = (values - high.astype(F32)).astype(BF16)
        lse = part_ref[rows, HDIM:]
        first = lse.astype(BF16).astype(F32)
        second = (lse - first).astype(BF16).astype(F32)
        third = lse - first - second
        lse = jnp.where(lane == 0, first, jnp.where(lane == 1, second, third))
        gift_ref[21 + half] = lse.astype(BF16)
    grad = jnp.zeros((BLK, HDIM), F32)
    for o in range(16):
        cot = cot_ref[o]
        grad = grad + dot(cot, w_ref[:, o * 256 : (o + 1) * 256], ((1,), (1,)))
        gift_ref[1 + o] = jnp.where(core == 0, cot[:, BLK:], cot[:, :BLK])
    gift_ref[0] = grad.astype(BF16)


def forward_kernel(q_ref, other_ref, kv0, kv1, kv2, kv3, part_ref, s_ref):
    pieces = (kv0, kv1, kv2, kv3)
    q = jnp.concatenate([q_ref[...], other_ref[...]], axis=0)
    top = jnp.full((2 * BLK, BLK), -jnp.inf, F32)
    for j in range(4):
        k = pieces[j][:, 0].reshape(WIDTH, HDIM)
        s = dot(q, k, ((1,), (1,))) * SCALE
        s_ref[:, j * WIDTH : (j + 1) * WIDTH] = s
        for t in range(4):
            top = jnp.maximum(top, s[:, t * BLK : (t + 1) * BLK])
    row_max = jnp.max(top, axis=1, keepdims=True)
    sums = jnp.zeros((2 * BLK, BLK), F32)
    acc = jnp.zeros((2 * BLK, HDIM), F32)
    for j in range(4):
        p = jnp.exp(s_ref[:, j * WIDTH : (j + 1) * WIDTH] - row_max)
        for t in range(4):
            sums = sums + p[:, t * BLK : (t + 1) * BLK]
        v = pieces[j][:, 1].reshape(WIDTH, HDIM)
        acc = acc + dot(p.astype(BF16), v)
    totals = jnp.sum(sums, axis=1, keepdims=True)
    part_ref[:, :HDIM] = acc / totals
    part_ref[:, HDIM:] = jnp.broadcast_to(row_max + jnp.log(totals), (2 * BLK, BLK))


def merged(grad, mine_ref, got_ref, half):
    rows = slice(half * BLK, (half + 1) * BLK)
    swapped = 1 - half
    parts = got_ref[21 + swapped].astype(F32)
    b = parts[:, :1] + parts[:, 1:2] + parts[:, 2:3]
    a = mine_ref[rows, HDIM : HDIM + 1]
    top = jnp.maximum(a, b)
    lse = top + jnp.log(jnp.exp(a - top) + jnp.exp(b - top))
    theirs = got_ref[17 + 2 * swapped].astype(F32) + got_ref[18 + 2 * swapped].astype(F32)
    attn = mine_ref[rows, :HDIM] * jnp.exp(a - lse)
    attn = (attn + theirs * jnp.exp(b - lse)).astype(BF16)
    dots = jnp.sum(grad.astype(F32) * attn.astype(F32), axis=1, keepdims=True)
    return grad, attn, lse, dots


def backward_kernel(
    place_ref, q_ref, other_ref, kv0, kv1, kv2, kv3, cot_ref, w_ref, gift_ref, got_ref, mine_ref, *refs
):
    pieces = (kv0, kv1, kv2, kv3)
    dq_ref, pay_hbm, *out_hbm, pay_ref, out_ref, sems = refs
    halves = [
        merged(ref[0], mine_ref, got_ref, half) for half, ref in enumerate((gift_ref, got_ref))
    ]
    mine = pl.ds(pl.multiple_of(place_ref[0] * BLK, BLK), BLK)
    grad, attn, lse, dots = (jnp.concatenate(pair, axis=0) for pair in zip(*halves))
    copies = []
    for r in range(4):
        for t in range(4):
            o = lax.bitwise_xor(place_ref[2], t) * 4 + lax.bitwise_xor(place_ref[3], r)
            cols = pl.ds(pl.multiple_of(o * 256, 256), 256)
            out_ref[r, t] = dot(halves[0][1], w_ref[:, cols]).astype(BF16)
        copies.append(pltpu.make_async_copy(out_ref.at[r], out_hbm[r], sems.at[r]))
        copies[r].start()
    q = jnp.concatenate([q_ref[...], other_ref[...]], axis=0)
    q_t = q.T
    grad_t = grad.T
    attn_t = attn.T
    dq = jnp.zeros((2 * BLK, HDIM), F32)
    for j in range(4):
        x = lax.bitwise_xor(place_ref[1], j)
        k = pieces[j][:, 0].reshape(WIDTH, HDIM)
        v = pieces[j][:, 1].reshape(WIDTH, HDIM)
        s = dot(q, k, ((1,), (1,))) * SCALE
        p = jnp.exp(s - lse)
        dp = dot(grad, v, ((1,), (1,)))
        ds = (p * (dp - dots)).astype(BF16)
        dq = dq + dot(ds, k)
        dk_t = dot(q_t, ds).astype(BF16)
        dv_t = dot(grad_t, p.astype(BF16)).astype(BF16)
        for z in range(4):
            pay_ref[j, z, 0] = dk_t[:, z * BLK : (z + 1) * BLK]
            pay_ref[j, z, 1] = dv_t[:, z * BLK : (z + 1) * BLK]
            o = z * 4 + x
            cot = jnp.concatenate([cot_ref[o, :, mine], got_ref[1 + o]], axis=0)
            pay_ref[j, z, 2] = dot(attn_t, cot).astype(BF16)
        copies.append(pltpu.make_async_copy(pay_ref.at[j], pay_hbm.at[x], sems.at[4 + j]))
        copies[4 + j].start()
    dq_ref[0] = dq[:BLK]
    dq_ref[1] = dq[BLK:]
    for copy in copies:
        copy.wait()


def finish_kernel(parts_ref, dk_ref, dv_ref, dw_ref):
    total = jnp.sum(parts_ref[...].astype(F32), axis=0)
    dk_ref[...] = (total[0] * SCALE).T.astype(BF16)
    dv_ref[...] = total[1].T.astype(BF16)
    dw_ref[...] = total[2]


def exchange(blocks, axis):
    return lax.all_to_all(blocks, axis, 0, 0, tiled=True)


def trade(block, axis, step):
    return lax.ppermute(block, axis, [(i, i ^ step) for i in range(2 if axis == "c" else 4)])


def in_hbm(block):
    return pltpu.with_memory_space_constraint(block, pltpu.HBM)


def add_all(blocks):
    total = blocks[0].astype(F32)
    for block in blocks[1:]:
        total = total + block.astype(F32)
    return total


def call(kernel, name, out_shape, in_specs, limit, flops, nbytes, exps=0, scratch=(), out_specs=None):
    return pl.pallas_call(
        kernel,
        out_shape=out_shape,
        in_specs=in_specs,
        out_specs=jax.tree.map(lambda _: VMEM, out_shape) if out_specs is None else out_specs,
        scratch_shapes=scratch,
        compiler_params=pltpu.CompilerParams(vmem_limit_bytes=limit << 20),
        cost_estimate=pl.CostEstimate(flops=flops, bytes_accessed=nbytes, transcendentals=exps),
        name=name,
    )


def body(queries, keys, values, w_out, grad_out):
    unit = BLK * BLK * 4096
    tile = shape((BLK, BLK), BF16)
    place = jnp.stack([lax.axis_index(a) for a in ("c", "x", "y", "zl")]).astype(jnp.int32)
    kv, cot = call(
        pack_kernel,
        "pack",
        (shape((2 * BLK, HDIM), BF16), shape((BLK, 2 * BLK), BF16)),
        [HBM] * 3,
        4,
        0,
        1 << 18,
        scratch=[pltpu.SemaphoreType.DMA((3,))],
    )(in_hbm(keys), in_hbm(values), in_hbm(grad_out))
    kv = lax.all_gather(kv, "zh", axis=0, tiled=True).reshape(4, 2, BLK, HDIM)
    kv, gift, cot, place = lax.optimization_barrier((kv, queries, cot, place))
    cot = exchange(jnp.broadcast_to(cot[None], (16, BLK, 2 * BLK)), ("y", "zl"))
    other = trade(gift, "c", 1)
    pieces = [kv] + [trade(kv, "x", r) for r in (1, 2, 3)]
    part = call(
        forward_kernel,
        "forward",
        shape((2 * BLK, 2 * BLK), F32),
        [VMEM] * 6,
        8,
        4 * unit,
        4 << 20,
        unit // BLK,
        [pltpu.VMEM((2 * BLK, 16 * BLK), F32)],
    )(queries, other, *pieces)
    cot, part = lax.optimization_barrier((cot, part))
    gift = call(
        cotangent_kernel,
        "cotangent",
        shape((23, BLK, BLK), BF16),
        [SMEM] + [VMEM] * 3,
        8,
        2 * unit,
        2 << 20,
    )(place, w_out, cot, part)
    got = trade(gift, "c", 1)
    dq, pay, *outs = call(
        backward_kernel,
        "backward",
        (shape((2, BLK, HDIM), F32), pltpu.HBM((4, 4, 3, BLK, BLK), BF16))
        + (pltpu.HBM((4, BLK, 256), BF16),) * 4,
        [SMEM] + [VMEM] * 11,
        12,
        14 * unit,
        8 << 20,
        unit // BLK,
        [
            pltpu.VMEM((4, 4, 3, BLK, BLK), BF16),
            pltpu.VMEM((4, 4, BLK, 256), BF16),
            pltpu.SemaphoreType.DMA((8,)),
        ],
        (VMEM,) + (HBM,) * 5,
    )(place, queries, other, *pieces, cot, w_out, gift, got, part)
    pay, *outs = lax.optimization_barrier((pay, *outs))
    pay = exchange(pay, "x")
    passing = trade(outs[3], "zl", 1)
    near = trade(outs[1], "zl", 1)
    dq_got = trade(dq[1], "c", 1)
    passing, dq_got = lax.optimization_barrier((passing, dq_got))
    far = trade(add_all([outs[2], passing]).astype(BF16), "zl", 2)
    pay = add_all([pay[r] for r in range(4)]).astype(BF16)
    pay = exchange(pay, "zh")
    out = add_all([outs[0], near, far]).astype(BF16)
    out = add_all([out[0]] + [trade(out[t], "y", t) for t in (1, 2, 3)]).astype(BF16)
    dq = ((dq[0] + dq_got) * SCALE).astype(BF16)
    dk, dv, dw = call(
        finish_kernel, "finish", (tile, tile, shape((BLK, BLK), F32)), [VMEM], 4, 0, 1 << 20
    )(pay)
    return out, dq, dk, dv, dw


def solution(mesh):
    fine = Mesh(mesh.devices.reshape(4, 4, 4, 4, 2), ("y", "zl", "zh", "x", "c"))
    outer, inner = ("y", "zl"), ("zh", "x", "c")
    spread = P(inner, outer)
    return jax.shard_map(
        body,
        mesh=fine,
        in_specs=(spread, spread, spread, P(outer, None), spread),
        out_specs=(spread, spread, spread, spread, P(outer, inner)),
        check_vma=False,
    )
```

```python
import jax
import jax.numpy as jnp
from jax import lax
from jax.experimental import pallas as pl
from jax.experimental.pallas import tpu as pltpu
from jax.sharding import Mesh, PartitionSpec as P

HDIM = 128
BLK = 128
WIDTH = 4 * BLK
SCALE = HDIM ** (-0.5)
F32 = jnp.float32
BF16 = jnp.bfloat16
VMEM = pl.BlockSpec(memory_space=pltpu.VMEM)
SMEM = pl.BlockSpec(memory_space=pltpu.SMEM)
HBM = pl.BlockSpec(memory_space=pltpu.HBM)
shape = jax.ShapeDtypeStruct


def dot(a, b, dims=((1,), (0,))):
    return lax.dot_general(a, b, (dims, ((), ())), preferred_element_type=F32)


def pack_kernel(k_hbm, v_hbm, grad_hbm, kv_ref, grad_ref, sems):
    copies = [
        pltpu.make_async_copy(grad_hbm, grad_ref, sems.at[2]),
        pltpu.make_async_copy(k_hbm, kv_ref.at[pl.ds(0, BLK)], sems.at[0]),
        pltpu.make_async_copy(v_hbm, kv_ref.at[pl.ds(BLK, BLK)], sems.at[1]),
    ]
    for copy in copies:
        copy.start()
    for copy in copies:
        copy.wait()


def cotangent_kernel(place_ref, w_ref, cot_ref, gift_ref):
    core = place_ref[0]
    grad = jnp.zeros((BLK, HDIM), F32)
    for o in range(16):
        cot = cot_ref[o]
        grad = grad + dot(cot, w_ref[:, o * 256 : (o + 1) * 256], ((1,), (1,)))
        gift_ref[1 + o] = jnp.where(core == 0, cot[:, BLK:], cot[:, :BLK])
    gift_ref[0] = grad.astype(BF16)


def forward_kernel(q_ref, other_ref, kv0, kv1, kv2, kv3, part_ref, s_ref):
    pieces = (kv0, kv1, kv2, kv3)
    q = jnp.concatenate([q_ref[...], other_ref[...]], axis=0)
    top = jnp.full((2 * BLK, BLK), -jnp.inf, F32)
    for j in range(4):
        k = pieces[j][:, 0].reshape(WIDTH, HDIM)
        s = dot(q, k, ((1,), (1,))) * SCALE
        s_ref[:, j * WIDTH : (j + 1) * WIDTH] = s
        for t in range(4):
            top = jnp.maximum(top, s[:, t * BLK : (t + 1) * BLK])
    row_max = jnp.max(top, axis=1, keepdims=True)
    sums = jnp.zeros((2 * BLK, BLK), F32)
    acc = jnp.zeros((2 * BLK, HDIM), F32)
    for j in range(4):
        p = jnp.exp(s_ref[:, j * WIDTH : (j + 1) * WIDTH] - row_max)
        for t in range(4):
            sums = sums + p[:, t * BLK : (t + 1) * BLK]
        v = pieces[j][:, 1].reshape(WIDTH, HDIM)
        acc = acc + dot(p.astype(BF16), v)
    totals = jnp.sum(sums, axis=1, keepdims=True)
    part_ref[:, :HDIM] = acc / totals
    part_ref[:, HDIM:] = jnp.broadcast_to(row_max + jnp.log(totals), (2 * BLK, BLK))


def merged(grad, mine_ref, theirs_ref, half):
    rows = slice(half * BLK, (half + 1) * BLK)
    swapped = slice((1 - half) * BLK, (2 - half) * BLK)
    a, b = mine_ref[rows, HDIM:], theirs_ref[swapped, HDIM:]
    top = jnp.maximum(a, b)
    lse = top + jnp.log(jnp.exp(a - top) + jnp.exp(b - top))
    attn = mine_ref[rows, :HDIM] * jnp.exp(a - lse)
    attn = (attn + theirs_ref[swapped, :HDIM] * jnp.exp(b - lse)).astype(BF16)
    dots = jnp.sum(grad.astype(F32) * attn.astype(F32), axis=1, keepdims=True)
    return grad, attn, lse[:, :1], dots


def backward_kernel(
    place_ref, q_ref, other_ref, kv0, kv1, kv2, kv3, cot_ref, w_ref, gift_ref, got_ref, mine_ref, theirs_ref, *refs
):
    pieces = (kv0, kv1, kv2, kv3)
    dq_ref, pay_hbm, *out_hbm, pay_ref, out_ref, sems = refs
    halves = [
        merged(ref[0], mine_ref, theirs_ref, half) for half, ref in enumerate((gift_ref, got_ref))
    ]
    mine = pl.ds(pl.multiple_of(place_ref[0] * BLK, BLK), BLK)
    grad, attn, lse, dots = (jnp.concatenate(pair, axis=0) for pair in zip(*halves))
    copies = []
    for r in range(4):
        for t in range(4):
            o = lax.bitwise_xor(place_ref[2], t) * 4 + lax.bitwise_xor(place_ref[3], r)
            cols = pl.ds(pl.multiple_of(o * 256, 256), 256)
            out_ref[r, t] = dot(halves[0][1], w_ref[:, cols]).astype(BF16)
        copies.append(pltpu.make_async_copy(out_ref.at[r], out_hbm[r], sems.at[r]))
        copies[r].start()
    q = jnp.concatenate([q_ref[...], other_ref[...]], axis=0)
    q_t = q.T
    grad_t = grad.T
    attn_t = attn.T
    dq = jnp.zeros((2 * BLK, HDIM), F32)
    for j in range(4):
        x = lax.bitwise_xor(place_ref[1], j)
        k = pieces[j][:, 0].reshape(WIDTH, HDIM)
        v = pieces[j][:, 1].reshape(WIDTH, HDIM)
        s = dot(q, k, ((1,), (1,))) * SCALE
        p = jnp.exp(s - lse)
        dp = dot(grad, v, ((1,), (1,)))
        ds = (p * (dp - dots)).astype(BF16)
        dq = dq + dot(ds, k)
        dk_t = dot(q_t, ds).astype(BF16)
        dv_t = dot(grad_t, p.astype(BF16)).astype(BF16)
        for z in range(4):
            pay_ref[j, z, 0] = dk_t[:, z * BLK : (z + 1) * BLK]
            pay_ref[j, z, 1] = dv_t[:, z * BLK : (z + 1) * BLK]
            o = z * 4 + x
            cot = jnp.concatenate([cot_ref[o, :, mine], got_ref[1 + o]], axis=0)
            pay_ref[j, z, 2] = dot(attn_t, cot).astype(BF16)
        copies.append(pltpu.make_async_copy(pay_ref.at[j], pay_hbm.at[x], sems.at[4 + j]))
        copies[4 + j].start()
    dq_ref[0] = dq[:BLK]
    dq_ref[1] = dq[BLK:]
    for copy in copies:
        copy.wait()


def finish_kernel(parts_ref, dk_ref, dv_ref, dw_ref):
    total = jnp.sum(parts_ref[...].astype(F32), axis=0)
    dk_ref[...] = (total[0] * SCALE).T.astype(BF16)
    dv_ref[...] = total[1].T.astype(BF16)
    dw_ref[...] = total[2]


def exchange(blocks, axis):
    return lax.all_to_all(blocks, axis, 0, 0, tiled=True)


def trade(block, axis, step):
    return lax.ppermute(block, axis, [(i, i ^ step) for i in range(2 if axis == "c" else 4)])


def in_hbm(block):
    return pltpu.with_memory_space_constraint(block, pltpu.HBM)


def add_all(blocks):
    total = blocks[0].astype(F32)
    for block in blocks[1:]:
        total = total + block.astype(F32)
    return total


def call(kernel, name, out_shape, in_specs, limit, flops, nbytes, exps=0, scratch=(), out_specs=None):
    return pl.pallas_call(
        kernel,
        out_shape=out_shape,
        in_specs=in_specs,
        out_specs=jax.tree.map(lambda _: VMEM, out_shape) if out_specs is None else out_specs,
        scratch_shapes=scratch,
        compiler_params=pltpu.CompilerParams(vmem_limit_bytes=limit << 20),
        cost_estimate=pl.CostEstimate(flops=flops, bytes_accessed=nbytes, transcendentals=exps),
        name=name,
    )


def body(queries, keys, values, w_out, grad_out):
    unit = BLK * BLK * 4096
    tile = shape((BLK, BLK), BF16)
    place = jnp.stack([lax.axis_index(a) for a in ("c", "x", "y", "zl")]).astype(jnp.int32)
    kv, cot = call(
        pack_kernel,
        "pack",
        (shape((2 * BLK, HDIM), BF16), shape((BLK, 2 * BLK), BF16)),
        [HBM] * 3,
        4,
        0,
        1 << 18,
        scratch=[pltpu.SemaphoreType.DMA((3,))],
    )(in_hbm(keys), in_hbm(values), in_hbm(grad_out))
    kv = lax.all_gather(kv, "zh", axis=0, tiled=True).reshape(4, 2, BLK, HDIM)
    kv, gift, cot, place = lax.optimization_barrier((kv, queries, cot, place))
    cot = exchange(jnp.broadcast_to(cot[None], (16, BLK, 2 * BLK)), ("y", "zl"))
    other = trade(gift, "c", 1)
    pieces = [kv] + [trade(kv, "x", r) for r in (1, 2, 3)]
    part = call(
        forward_kernel,
        "forward",
        shape((2 * BLK, 2 * BLK), F32),
        [VMEM] * 6,
        8,
        4 * unit,
        4 << 20,
        unit // BLK,
        [pltpu.VMEM((2 * BLK, 16 * BLK), F32)],
    )(queries, other, *pieces)
    theirs = trade(part, "c", 1)
    cot, theirs = lax.optimization_barrier((cot, theirs))
    gift = call(
        cotangent_kernel,
        "cotangent",
        shape((17, BLK, BLK), BF16),
        [SMEM] + [VMEM] * 2,
        8,
        2 * unit,
        2 << 20,
    )(place, w_out, cot)
    got = trade(gift, "c", 1)
    dq, pay, *outs = call(
        backward_kernel,
        "backward",
        (shape((2, BLK, HDIM), F32), pltpu.HBM((4, 4, 3, BLK, BLK), BF16))
        + (pltpu.HBM((4, BLK, 256), BF16),) * 4,
        [SMEM] + [VMEM] * 12,
        12,
        14 * unit,
        8 << 20,
        unit // BLK,
        [
            pltpu.VMEM((4, 4, 3, BLK, BLK), BF16),
            pltpu.VMEM((4, 4, BLK, 256), BF16),
            pltpu.SemaphoreType.DMA((8,)),
        ],
        (VMEM,) + (HBM,) * 5,
    )(place, queries, other, *pieces, cot, w_out, gift, got, part, theirs)
    pay, *outs = lax.optimization_barrier((pay, *outs))
    pay = exchange(pay, "x")
    passing = trade(outs[3], "zl", 1)
    near = trade(outs[1], "zl", 1)
    far = trade(add_all([outs[2], passing]).astype(BF16), "zl", 2)
    pay = add_all([pay[r] for r in range(4)]).astype(BF16)
    pay = exchange(pay, "zh")
    out = add_all([outs[0], near, far]).astype(BF16)
    out = add_all([out[0]] + [trade(out[t], "y", t) for t in (1, 2, 3)]).astype(BF16)
    dq = ((dq[0] + trade(dq[1], "c", 1)) * SCALE).astype(BF16)
    dk, dv, dw = call(
        finish_kernel, "finish", (tile, tile, shape((BLK, BLK), F32)), [VMEM], 4, 0, 1 << 20
    )(pay)
    return out, dq, dk, dv, dw


def solution(mesh):
    fine = Mesh(mesh.devices.reshape(4, 4, 4, 4, 2), ("y", "zl", "zh", "x", "c"))
    outer, inner = ("y", "zl"), ("zh", "x", "c")
    spread = P(inner, outer)
    return jax.shard_map(
        body,
        mesh=fine,
        in_specs=(spread, spread, spread, P(outer, None), spread),
        out_specs=(spread, spread, spread, spread, P(outer, inner)),
        check_vma=False,
    )
```

```python
import jax
import jax.numpy as jnp
from jax import lax
from jax.experimental import pallas as pl
from jax.experimental.pallas import tpu as pltpu
from jax.sharding import Mesh, PartitionSpec as P

HDIM = 128
BLK = 128
WIDTH = 4 * BLK
SCALE = HDIM ** (-0.5)
F32 = jnp.float32
BF16 = jnp.bfloat16
VMEM = pl.BlockSpec(memory_space=pltpu.VMEM)
SMEM = pl.BlockSpec(memory_space=pltpu.SMEM)
HBM = pl.BlockSpec(memory_space=pltpu.HBM)
shape = jax.ShapeDtypeStruct


def dot(a, b, dims=((1,), (0,))):
    return lax.dot_general(a, b, (dims, ((), ())), preferred_element_type=F32)


def pack_kernel(k_hbm, v_hbm, grad_hbm, kv_ref, grad_ref, sems):
    copies = [
        pltpu.make_async_copy(grad_hbm, grad_ref, sems.at[2]),
        pltpu.make_async_copy(k_hbm, kv_ref.at[pl.ds(0, BLK)], sems.at[0]),
        pltpu.make_async_copy(v_hbm, kv_ref.at[pl.ds(BLK, BLK)], sems.at[1]),
    ]
    for copy in copies:
        copy.start()
    for copy in copies:
        copy.wait()


def cotangent_kernel(place_ref, w_ref, cot_ref, gift_ref):
    core = place_ref[0]
    grad = jnp.zeros((BLK, HDIM), F32)
    for o in range(16):
        cot = cot_ref[o]
        grad = grad + dot(cot, w_ref[:, o * 256 : (o + 1) * 256], ((1,), (1,)))
        gift_ref[1 + o] = jnp.where(core == 0, cot[:, BLK:], cot[:, :BLK])
    gift_ref[0] = grad.astype(BF16)


def forward_kernel(q_ref, other_ref, kv0, kv1, kv2, kv3, part_ref, s_ref):
    pieces = (kv0, kv1, kv2, kv3)
    q = jnp.concatenate([q_ref[...], other_ref[...]], axis=0)
    top = jnp.full((2 * BLK, BLK), -jnp.inf, F32)
    for j in range(4):
        k = pieces[j][:, 0].reshape(WIDTH, HDIM)
        s = dot(q, k, ((1,), (1,))) * SCALE
        s_ref[:, j * WIDTH : (j + 1) * WIDTH] = s
        for t in range(4):
            top = jnp.maximum(top, s[:, t * BLK : (t + 1) * BLK])
    row_max = jnp.max(top, axis=1, keepdims=True)
    sums = jnp.zeros((2 * BLK, BLK), F32)
    acc = jnp.zeros((2 * BLK, HDIM), F32)
    for j in range(4):
        p = jnp.exp(s_ref[:, j * WIDTH : (j + 1) * WIDTH] - row_max)
        for t in range(4):
            sums = sums + p[:, t * BLK : (t + 1) * BLK]
        v = pieces[j][:, 1].reshape(WIDTH, HDIM)
        acc = acc + dot(p.astype(BF16), v)
    totals = jnp.sum(sums, axis=1, keepdims=True)
    part_ref[:, :HDIM] = acc / totals
    part_ref[:, HDIM:] = jnp.broadcast_to(row_max + jnp.log(totals), (2 * BLK, BLK))


def merged(grad, mine_ref, theirs_ref, half):
    rows = slice(half * BLK, (half + 1) * BLK)
    swapped = slice((1 - half) * BLK, (2 - half) * BLK)
    a, b = mine_ref[rows, HDIM:], theirs_ref[swapped, HDIM:]
    top = jnp.maximum(a, b)
    lse = top + jnp.log(jnp.exp(a - top) + jnp.exp(b - top))
    attn = mine_ref[rows, :HDIM] * jnp.exp(a - lse)
    attn = (attn + theirs_ref[swapped, :HDIM] * jnp.exp(b - lse)).astype(BF16)
    dots = jnp.sum(grad.astype(F32) * attn.astype(F32), axis=1, keepdims=True)
    return grad, attn, lse[:, :1], dots


def backward_kernel(
    place_ref, q_ref, other_ref, kv0, kv1, kv2, kv3, cot_ref, w_ref, gift_ref, got_ref, mine_ref, theirs_ref, *refs
):
    pieces = (kv0, kv1, kv2, kv3)
    dq_ref, pay_hbm, *out_hbm, pay_ref, out_ref, sems = refs
    halves = [
        merged(ref[0], mine_ref, theirs_ref, half) for half, ref in enumerate((gift_ref, got_ref))
    ]
    mine = pl.ds(pl.multiple_of(place_ref[0] * BLK, BLK), BLK)
    grad, attn, lse, dots = (jnp.concatenate(pair, axis=0) for pair in zip(*halves))
    copies = []
    for r in range(4):
        for t in range(4):
            o = lax.bitwise_xor(place_ref[2], t) * 4 + lax.bitwise_xor(place_ref[3], r)
            cols = pl.ds(pl.multiple_of(o * 256, 256), 256)
            out_ref[r, t] = dot(halves[0][1], w_ref[:, cols]).astype(BF16)
        copies.append(pltpu.make_async_copy(out_ref.at[r], out_hbm[r], sems.at[r]))
        copies[r].start()
    q = jnp.concatenate([q_ref[...], other_ref[...]], axis=0)
    q_t = q.T
    grad_t = grad.T
    attn_t = attn.T
    dq = jnp.zeros((2 * BLK, HDIM), F32)
    for j in range(4):
        x = lax.bitwise_xor(place_ref[1], j)
        k = pieces[j][:, 0].reshape(WIDTH, HDIM)
        v = pieces[j][:, 1].reshape(WIDTH, HDIM)
        s = dot(q, k, ((1,), (1,))) * SCALE
        p = jnp.exp(s - lse)
        dp = dot(grad, v, ((1,), (1,)))
        ds = (p * (dp - dots)).astype(BF16)
        dq = dq + dot(ds, k)
        dk_t = dot(q_t, ds).astype(BF16)
        dv_t = dot(grad_t, p.astype(BF16)).astype(BF16)
        for z in range(4):
            pay_ref[j, z, 0] = dk_t[:, z * BLK : (z + 1) * BLK]
            pay_ref[j, z, 1] = dv_t[:, z * BLK : (z + 1) * BLK]
            o = z * 4 + x
            cot = jnp.concatenate([cot_ref[o, :, mine], got_ref[1 + o]], axis=0)
            pay_ref[j, z, 2] = dot(attn_t, cot).astype(BF16)
        copies.append(pltpu.make_async_copy(pay_ref.at[j], pay_hbm.at[x], sems.at[4 + j]))
        copies[4 + j].start()
    dq_ref[0] = dq[:BLK]
    dq_ref[1] = dq[BLK:]
    for copy in copies:
        copy.wait()


def finish_kernel(parts_ref, dk_ref, dv_ref, dw_ref):
    total = jnp.sum(parts_ref[...].astype(F32), axis=0)
    dk_ref[...] = (total[0] * SCALE).T.astype(BF16)
    dv_ref[...] = total[1].T.astype(BF16)
    dw_ref[...] = total[2]


def exchange(blocks, axis):
    return lax.all_to_all(blocks, axis, 0, 0, tiled=True)


def trade(block, axis, step):
    return lax.ppermute(block, axis, [(i, i ^ step) for i in range(2 if axis == "c" else 4)])


def in_hbm(block):
    return pltpu.with_memory_space_constraint(block, pltpu.HBM)


def add_all(blocks):
    total = blocks[0].astype(F32)
    for block in blocks[1:]:
        total = total + block.astype(F32)
    return total


def call(kernel, name, out_shape, in_specs, limit, flops, nbytes, exps=0, scratch=(), out_specs=None):
    return pl.pallas_call(
        kernel,
        out_shape=out_shape,
        in_specs=in_specs,
        out_specs=jax.tree.map(lambda _: VMEM, out_shape) if out_specs is None else out_specs,
        scratch_shapes=scratch,
        compiler_params=pltpu.CompilerParams(vmem_limit_bytes=limit << 20),
        cost_estimate=pl.CostEstimate(flops=flops, bytes_accessed=nbytes, transcendentals=exps),
        name=name,
    )


def body(queries, keys, values, w_out, grad_out):
    unit = BLK * BLK * 4096
    tile = shape((BLK, BLK), BF16)
    place = jnp.stack([lax.axis_index(a) for a in ("c", "x", "y", "zl")]).astype(jnp.int32)
    kv, cot = call(
        pack_kernel,
        "pack",
        (shape((2 * BLK, HDIM), BF16), shape((BLK, 2 * BLK), BF16)),
        [HBM] * 3,
        4,
        0,
        1 << 18,
        scratch=[pltpu.SemaphoreType.DMA((3,))],
    )(in_hbm(keys), in_hbm(values), in_hbm(grad_out))
    kv = lax.all_gather(kv, "zh", axis=0, tiled=True).reshape(4, 2, BLK, HDIM)
    kv, gift, cot, place = lax.optimization_barrier((kv, queries, cot, place))
    cot = exchange(jnp.broadcast_to(cot[None], (16, BLK, 2 * BLK)), ("y", "zl"))
    other = trade(gift, "c", 1)
    pieces = [kv] + [trade(kv, "x", r) for r in (1, 2, 3)]
    part = call(
        forward_kernel,
        "forward",
        shape((2 * BLK, 2 * BLK), F32),
        [VMEM] * 6,
        8,
        4 * unit,
        4 << 20,
        unit // BLK,
        [pltpu.VMEM((2 * BLK, 16 * BLK), F32)],
    )(queries, other, *pieces)
    theirs = trade(part, "c", 1)
    cot, theirs = lax.optimization_barrier((cot, theirs))
    gift = call(
        cotangent_kernel,
        "cotangent",
        shape((17, BLK, BLK), BF16),
        [SMEM] + [VMEM] * 2,
        8,
        2 * unit,
        2 << 20,
    )(place, w_out, cot)
    got = trade(gift, "c", 1)
    dq, pay, *outs = call(
        backward_kernel,
        "backward",
        (shape((2, BLK, HDIM), F32), pltpu.HBM((4, 4, 3, BLK, BLK), BF16))
        + (pltpu.HBM((4, BLK, 256), BF16),) * 4,
        [SMEM] + [VMEM] * 12,
        12,
        14 * unit,
        8 << 20,
        unit // BLK,
        [
            pltpu.VMEM((4, 4, 3, BLK, BLK), BF16),
            pltpu.VMEM((4, 4, BLK, 256), BF16),
            pltpu.SemaphoreType.DMA((8,)),
        ],
        (VMEM,) + (HBM,) * 5,
    )(place, queries, other, *pieces, cot, w_out, gift, got, part, theirs)
    pay, *outs = lax.optimization_barrier((pay, *outs))
    pay = exchange(pay, "x")
    passing = trade(outs[3], "zl", 1)
    near = trade(outs[1], "zl", 1)
    dq_got = trade(dq[1], "c", 1)
    pay, dq_got = lax.optimization_barrier((pay, dq_got))
    far = trade(add_all([outs[2], passing]).astype(BF16), "zl", 2)
    pay = add_all([pay[r] for r in range(4)]).astype(BF16)
    pay = exchange(pay, "zh")
    out = add_all([outs[0], near, far]).astype(BF16)
    out = add_all([out[0]] + [trade(out[t], "y", t) for t in (1, 2, 3)]).astype(BF16)
    dq = ((dq[0] + dq_got) * SCALE).astype(BF16)
    dk, dv, dw = call(
        finish_kernel, "finish", (tile, tile, shape((BLK, BLK), F32)), [VMEM], 4, 0, 1 << 20
    )(pay)
    return out, dq, dk, dv, dw


def solution(mesh):
    fine = Mesh(mesh.devices.reshape(4, 4, 4, 4, 2), ("y", "zl", "zh", "x", "c"))
    outer, inner = ("y", "zl"), ("zh", "x", "c")
    spread = P(inner, outer)
    return jax.shard_map(
        body,
        mesh=fine,
        in_specs=(spread, spread, spread, P(outer, None), spread),
        out_specs=(spread, spread, spread, spread, P(outer, inner)),
        check_vma=False,
    )
```
